32 devices in a mesh: group: 2 (over y), feat: 4 (over z), tok: 2 (over x), sub: 2 (over core).
Axes of the slice: x: 2, y: 2, z: 4, core: 2. Of those that a mesh axis runs over, the one named last changes fastest.
Arguments:
- inputs: bfloat16 [2048, 8192], P(('group', 'tok', 'sub'), 'feat'), parts along dimension 0, may hold values from -6 to 6
- cotangent: bfloat16 [2048, 8192], P(('group', 'tok', 'sub'), 'feat'), parts along dimension 0, may hold values from -6 to 6
- w_in: bfloat16 [64, 7, 128, 128], P('feat'), may hold values from -0.1875 to 0.1875
- w_out: bfloat16 [64, 7, 128, 128], P('feat'), may hold values from -0.1875 to 0.1875
- u_in: bfloat16 [8192, 128], P('feat'), may hold values from -0.0625 to 0.0625
- v_in: bfloat16 [128, 8192], P(None, 'feat'), may hold values from -0.5 to 0.5
- u_out: bfloat16 [8192, 128], P('feat'), may hold values from -0.0625 to 0.0625
- v_out: bfloat16 [128, 8192], P(None, 'feat'), may hold values from -0.5 to 0.5
Outputs:
- output: bfloat16 [2048, 8192], P(('group', 'tok', 'sub'), 'feat'), parts along dimension 0
- input_grad: bfloat16 [2048, 8192], P(('group', 'tok', 'sub'), 'feat'), parts along dimension 0
- grad_w_in: float32 [128, 7, 128, 128], P(('group', 'feat'), None, ('tok', 'sub')), parts along dimension 0
- grad_w_out: float32 [128, 7, 128, 128], P(('group', 'feat'), None, ('tok', 'sub')), parts along dimension 0
- grad_u_in: float32 [16384, 128], P(('group', 'feat'), ('tok', 'sub')), parts along dimension 0
- grad_v_in: float32 [256, 8192], P(('group', 'tok', 'sub'), 'feat'), parts along dimension 0
- grad_u_out: float32 [16384, 128], P(('group', 'feat'), ('tok', 'sub')), parts along dimension 0
- grad_v_out: float32 [256, 8192], P(('group', 'tok', 'sub'), 'feat'), parts along dimension 0
The draws below stay inside these ranges and needn't reach their ends.
There are 2 independent parts, one for each index of `group`. The reference program is written for one: setup_inputs(seed, part) draws one part's arguments, and reference() takes and returns one part's arrays. A program takes and returns all parts, laid end to end along the dimension named above; an argument that names none is the same for every part. Nothing has to cross between parts.
All inputs are finite; a program needn't handle non-finite values.
Results may differ from the reference program's by a relative error of at most 0.023.
Values may be sent and summed in bfloat16 or wider, within the bound.
No kernel may reach another device: no remote copies, remote signals or barrier semaphores. Data moves between devices by JAX's collectives and lax.ppermute only.
A program may use at most 192 MiB of HBM per device.

```python
import math
import jax
import jax.numpy as jnp
from jax import lax

D = 8192
HID = 8192
BLK = 128
SLOTS = 7
RANK = 128
TOK_DEV = 256
TOKENS = 1024
N_TOK = 2
N_SUB = 2


def block_scale(rng, dims, cuts, low, largest):
    gain = 1.0
    for axis_at, shards_of in cuts:
        heights = jax.random.uniform(jax.random.fold_in(jax.random.fold_in(rng, 6), axis_at), (shards_of,), jnp.float32, low / len(cuts), largest / len(cuts))
        gain = gain * jnp.repeat(jnp.exp(heights), dims[axis_at] // shards_of).reshape((-1,) + (1,) * (len(dims) - 1 - axis_at))
    return gain


def bell_draw(own_key, extent, deviation, most, split=(), kind=jnp.bfloat16):
    level = block_scale(own_key, extent, split, -0.22, 0.18) if split else 1.0
    array = jax.random.normal(own_key, extent, jnp.float32) * deviation * level
    return jnp.minimum(jnp.maximum(array, -most), most).astype(kind)


def setup_inputs(seed: int = 0, part: int = 0) -> dict:
    key_of = jax.random.split(jax.random.key(seed), 9)
    own_keys = jax.random.split(jax.random.fold_in(key_of[8], part), 9)
    inputs = bell_draw(own_keys[0], (TOKENS, D), 1.0, 6.0, ((0, 4), (1, 4)))
    cotangent = bell_draw(own_keys[1], (TOKENS, D), 1.0, 6.0, ((0, 4), (1, 4)))
    w_in = bell_draw(key_of[2], (HID // BLK, SLOTS, BLK, BLK), (SLOTS * BLK) ** -0.5, 0.1875, ((0, 4),))
    w_out = bell_draw(key_of[3], (D // BLK, SLOTS, BLK, BLK), (SLOTS * BLK) ** -0.5, 0.1875, ((0, 4),))
    u_in = bell_draw(key_of[4], (D, RANK), D ** -0.5, 0.0625, ((0, 4),))
    v_in = bell_draw(key_of[5], (RANK, HID), RANK ** -0.5, 0.5, ((1, 4),))
    u_out = bell_draw(key_of[6], (HID, RANK), HID ** -0.5, 0.0625, ((0, 4),))
    v_out = bell_draw(key_of[7], (RANK, D), RANK ** -0.5, 0.5, ((1, 4),))
    return dict(inputs=inputs, cotangent=cotangent, w_in=w_in, w_out=w_out, u_in=u_in, v_in=v_in, u_out=u_out, v_out=v_out)


def flip_level(array_in, level, dim_index):
    count = array_in.shape[dim_index]
    stride = 1 << level
    shape = array_in.shape[:dim_index] + (count // (2 * stride), 2, stride) + array_in.shape[dim_index + 1:]
    folded = jnp.flip(array_in.reshape(shape), axis=dim_index + 1)
    return folded.reshape(array_in.shape)

def gelu_parts(pre):
    factor = math.sqrt(2.0 / math.pi)
    tangent = jnp.tanh(factor * (pre + 0.044715 * pre * pre * pre))
    active = 0.5 * pre * (1.0 + tangent)
    slope = 0.5 * (1.0 + tangent) + 0.5 * pre * (1.0 - tangent * tangent) * factor * (1.0 + 3.0 * 0.044715 * pre * pre)
    return (active, slope)

def stack_partners(blocks):
    parts = [blocks] + [flip_level(blocks, level, 1) for level in range(SLOTS - 1)]
    return jnp.stack(parts, axis=2)

def stack_weights(weights):
    parts = [weights[:, 0]] + [flip_level(weights[:, 1 + level], level, 0) for level in range(SLOTS - 1)]
    return jnp.stack(parts, axis=1)

def apply_fly(blocks, weights):
    return jnp.einsum('tisb,isbc->tic', stack_partners(blocks).astype(jnp.float32), weights.astype(jnp.float32))

def apply_back(grads, moved):
    return jnp.einsum('tisc,isbc->tib', stack_partners(grads).astype(jnp.float32), moved.astype(jnp.float32))

def fly_grad(blocks, grads):
    return jnp.einsum('tosb,toc->osbc', stack_partners(blocks).astype(jnp.float32), grads.astype(jnp.float32))

def round_trip(partial_value):
    return lax.optimization_barrier(partial_value.astype(jnp.bfloat16)).astype(jnp.float32)

def reference(inputs, cotangent, w_in, w_out, u_in, v_in, u_out, v_out):
    groups = N_TOK * N_SUB
    nblocks = D // BLK
    moved_in = stack_weights(w_in)
    moved_out = stack_weights(w_out)
    input_groups = inputs.reshape(groups, TOK_DEV, D)
    cot_groups = cotangent.reshape(groups, TOK_DEV, D)

    def one_group(carry, pair):
        rows_in, rows_cot = pair
        blocks_in = rows_in.reshape(TOK_DEV, nblocks, BLK)
        code_in = jnp.dot(rows_in, u_in, preferred_element_type=jnp.float32).astype(jnp.bfloat16)
        pre = apply_fly(blocks_in, w_in).reshape(TOK_DEV, D) + jnp.dot(code_in, v_in, preferred_element_type=jnp.float32)
        active, slope = gelu_parts(pre)
        act = active.astype(jnp.bfloat16)
        act_blocks = act.reshape(TOK_DEV, nblocks, BLK)
        code_out = jnp.dot(act, u_out, preferred_element_type=jnp.float32).astype(jnp.bfloat16)
        result = (apply_fly(act_blocks, w_out).reshape(TOK_DEV, D) + jnp.dot(code_out, v_out, preferred_element_type=jnp.float32)).astype(jnp.bfloat16)
        cot_blocks = rows_cot.reshape(TOK_DEV, nblocks, BLK)
        back_out = jnp.dot(rows_cot, v_out.T, preferred_element_type=jnp.float32).astype(jnp.bfloat16)
        act_grad = apply_back(cot_blocks, moved_out).reshape(TOK_DEV, D) + jnp.dot(back_out, u_out.T, preferred_element_type=jnp.float32)
        pre_grad = (act_grad * slope).astype(jnp.bfloat16)
        pre_blocks = pre_grad.reshape(TOK_DEV, nblocks, BLK)
        back_in = jnp.dot(pre_grad, v_in.T, preferred_element_type=jnp.float32).astype(jnp.bfloat16)
        in_grad = (apply_back(pre_blocks, moved_in).reshape(TOK_DEV, D) + jnp.dot(back_in, u_in.T, preferred_element_type=jnp.float32)).astype(jnp.bfloat16)
        partials = (fly_grad(blocks_in, pre_blocks), fly_grad(act_blocks, cot_blocks), jnp.dot(rows_in.T, back_in, preferred_element_type=jnp.float32), jnp.dot(code_in.T, pre_grad, preferred_element_type=jnp.float32), jnp.dot(act.T, back_out, preferred_element_type=jnp.float32), jnp.dot(code_out.T, rows_cot, preferred_element_type=jnp.float32))
        carry = tuple((total + round_trip(partial_value) for total, partial_value in zip(carry, partials)))
        return (carry, (result, in_grad))
    start = (jnp.zeros(w_in.shape, jnp.float32), jnp.zeros(w_out.shape, jnp.float32), jnp.zeros(u_in.shape, jnp.float32), jnp.zeros(v_in.shape, jnp.float32), jnp.zeros(u_out.shape, jnp.float32), jnp.zeros(v_out.shape, jnp.float32))
    sums, (results, in_grads) = lax.scan(one_group, start, (input_groups, cot_groups))
    return (results.reshape(TOKENS, D), in_grads.reshape(TOKENS, D), sums[0], sums[1], sums[2], sums[3], sums[4], sums[5])
```

```python
import functools
import math

import jax
import jax.numpy as jnp
from jax import lax
from jax.experimental import pallas as pl
from jax.experimental.pallas import tpu as pltpu
from jax.sharding import PartitionSpec as P

F32 = jnp.float32
BF16 = jnp.bfloat16
VMEM_LIMIT = 40 * 1024 * 1024


def exchange(value, axis, mask):
    pairs = [(source, source ^ mask) for source in range(lax.axis_size(axis))]
    return lax.ppermute(value, axis, pairs)


def gelu_parts(pre):
    factor = math.sqrt(2.0 / math.pi)
    square = pre * pre
    tangent = jnp.tanh(factor * (pre + 0.044715 * square * pre))
    active = 0.5 * pre * (1.0 + tangent)
    slope = 0.5 * (1.0 + tangent) + 0.5 * pre * (1.0 - tangent * tangent) * factor * (
        1.0 + 3.0 * 0.044715 * square
    )
    return (active, slope)


def dot(left, right):
    return jnp.dot(left, right, preferred_element_type=F32)


def dot_nt(left, right):
    return lax.dot_general(left, right, (((1,), (1,)), ((), ())), preferred_element_type=F32)


def dot_tn(left, right):
    return lax.dot_general(left, right, (((0,), (0,)), ((), ())), preferred_element_type=F32)


def whole(shape):
    return pl.BlockSpec(shape, lambda g: (0,) * len(shape))


def by_cols(rows, width):
    return pl.BlockSpec((rows, width), lambda g: (0, g))


def by_rows(height, cols):
    return pl.BlockSpec((height, cols), lambda g: (g, 0))


def shape_of(shape, dtype=BF16):
    return jax.ShapeDtypeStruct(shape, dtype)


def call(body, grid, ins, outs, out_shapes, scratch, flops, args, name):
    moved = sum(a.size * a.dtype.itemsize for a in args) + sum(
        math.prod(s.shape) * s.dtype.itemsize for s in out_shapes
    )
    return pl.pallas_call(
        body,
        grid=grid,
        in_specs=ins,
        out_specs=outs,
        out_shape=out_shapes,
        scratch_shapes=scratch,
        compiler_params=pltpu.CompilerParams(vmem_limit_bytes=VMEM_LIMIT),
        cost_estimate=pl.CostEstimate(flops=flops, bytes_accessed=moved, transcendentals=0),
        name=name,
    )(*args)


class Layer:
    def __init__(self, inputs, weights):
        self.rows, self.cols = inputs.shape
        self.blocks, self.slots, self.blk, _ = weights.shape
        self.local = self.blocks.bit_length() - 1
        self.far = self.slots - 1 - self.local
        self.group = min(4, self.blocks)
        self.steps = self.blocks // self.group
        self.width = self.group * self.blk
        self.rank = self.blk

    def cut(self, j):
        return slice(j * self.blk, (j + 1) * self.blk)

    def place(self, g, j, k):
        if k == 0:
            return g * self.group + j
        mask = 1 << (k - 1)
        if mask < self.group:
            return g * self.group + (j ^ mask)
        return (g ^ (mask // self.group)) * self.group + j

    def columns(self, ref, block):
        return ref[:, pl.ds(pl.multiple_of(block * self.blk, self.blk), self.blk)]

    def flops(self, per_block):
        return 2 * self.rows * self.blk * self.blk * self.blocks * per_block

    def first_codes(self, inputs, cotangent, u_in, v_out):
        def body(x_ref, c_ref, u_ref, v_ref, code_ref, back_ref):
            code_ref[...] = dot(x_ref[...], u_ref[...]).astype(BF16)
            back_ref[...] = dot_nt(c_ref[...], v_ref[...]).astype(BF16)

        return call(
            body,
            (1,),
            [whole(inputs.shape), whole(inputs.shape), whole(u_in.shape), whole(v_out.shape)],
            [whole((self.rows, self.rank))] * 2,
            [shape_of((self.rows, self.rank))] * 2,
            [],
            self.flops(2),
            (inputs, cotangent, u_in, v_out),
            "first_codes",
        )

    def far_products(self, grads, weights, after):
        def body(g_ref, w_ref, *refs):
            outs = refs[len(after) :]
            for j in range(self.group):
                block = g_ref[:, self.cut(j)]
                for k in range(self.far):
                    outs[k][:, self.cut(j)] = dot_nt(
                        block, w_ref[j, 1 + self.local + k]
                    ).astype(BF16)

        weight_spec = pl.BlockSpec(
            (self.group, self.slots, self.blk, self.blk), lambda g: (g, 0, 0, 0)
        )
        return call(
            body,
            (self.steps,),
            [by_cols(self.rows, self.width), weight_spec]
            + [pl.BlockSpec(memory_space=pl.ANY)] * len(after),
            [by_cols(self.rows, self.width)] * self.far,
            [shape_of((self.rows, self.cols))] * self.far,
            [],
            self.flops(self.far),
            (grads, weights, *after),
            "far_products",
        )

    def forward(self, acts, far_acts, weights, codes, v, finish, outs, out_shapes, extra, extra_specs, scratch, name):
        n_far, n_codes, n_extra = len(far_acts), len(codes), len(extra)

        def body(a_ref, *refs):
            far_refs, refs = refs[:n_far], refs[n_far:]
            w_ref, refs = refs[0], refs[1:]
            code_refs, refs = refs[:n_codes], refs[n_codes:]
            v_ref, refs = refs[0], refs[1:]
            g = pl.program_id(0)
            code = sum(ref[...].astype(F32) for ref in code_refs).astype(BF16)
            for j in range(self.group):
                parts = [
                    self.columns(a_ref, self.place(g, j, k)) for k in range(1 + self.local)
                ] + [ref[:, self.cut(j)] for ref in far_refs]
                stacked = jnp.concatenate(parts, axis=1)
                weight = w_ref[j].reshape(self.slots * self.blk, self.blk)
                total = dot(stacked, weight) + dot(code, v_ref[:, self.cut(j)])
                finish(g, j, total, refs)

        weight_spec = pl.BlockSpec(
            (self.group, self.slots, self.blk, self.blk), lambda g: (g, 0, 0, 0)
        )
        return call(
            body,
            (self.steps,),
            [whole(acts.shape)]
            + [by_cols(self.rows, self.width)] * n_far
            + [weight_spec]
            + [whole((self.rows, self.rank))] * n_codes
            + [by_cols(self.rank, self.width)]
            + extra_specs,
            outs,
            out_shapes,
            scratch,
            self.flops(self.slots + 2),
            (acts, *far_acts, weights, *codes, v, *extra),
            name,
        )

    def hidden(self, inputs, far_inputs, w_in, codes, v_in, u_out):
        def finish(g, j, pre, refs):
            u_ref, act_ref, slope_ref, code_ref, sum_ref = refs
            active, slope = gelu_parts(pre)
            act = active.astype(BF16)
            act_ref[:, self.cut(j)] = act
            slope_ref[:, self.cut(j)] = slope
            part = dot(act, u_ref[self.cut(j), :])
            if j == 0:
                sum_ref[...] = jnp.where(g == 0, part, sum_ref[...] + part)
            else:
                sum_ref[...] += part
            if j == self.group - 1:
                code_ref[...] = sum_ref[...].astype(BF16)

        return self.forward(
            inputs,
            far_inputs,
            w_in,
            codes,
            v_in,
            finish,
            [by_cols(self.rows, self.width)] * 2 + [whole((self.rows, self.rank))],
            [
                shape_of((self.rows, self.cols)),
                shape_of((self.rows, self.cols), F32),
                shape_of((self.rows, self.rank)),
            ],
            [u_out],
            [by_rows(self.width, self.rank)],
            [pltpu.VMEM((self.rows, self.rank), F32)],
            "hidden",
        )

    def result(self, act, far_acts, w_out, codes, v_out):
        def finish(g, j, total, refs):
            refs[0][:, self.cut(j)] = total.astype(BF16)

        return self.forward(
            act,
            far_acts,
            w_out,
            codes,
            v_out,
            finish,
            [by_cols(self.rows, self.width)],
            [shape_of((self.rows, self.cols))],
            [],
            [],
            [],
            "result",
        )[0]

    def backward(self, grads, weights, codes, u, far_parts, finish, outs, out_shapes, extra, extra_specs, scratch, name):
        n_far, n_codes, n_extra = len(far_parts), len(codes), len(extra)

        def body(g_ref, w_ref, *refs):
            code_refs, refs = refs[:n_codes], refs[n_codes:]
            u_ref, refs = refs[0], refs[1:]
            far_refs, refs = refs[:n_far], refs[n_far:]
            g = pl.program_id(0)
            code = sum(ref[...].astype(F32) for ref in code_refs).astype(BF16)
            for j in range(self.group):
                places = [self.place(g, j, k) for k in range(1 + self.local)]
                stacked = jnp.concatenate(
                    [self.columns(g_ref, place) for place in places] + [code], axis=1
                )
                weight = jnp.concatenate(
                    [w_ref[place, k] for k, place in enumerate(places)] + [u_ref[self.cut(j), :]],
                    axis=1,
                )
                total = dot_nt(stacked, weight)
                for ref in far_refs:
                    total = total + ref[:, self.cut(j)].astype(F32)
                finish(g, j, total, refs)

        return call(
            body,
            (self.steps,),
            [whole(grads.shape), whole(weights.shape)]
            + [whole((self.rows, self.rank))] * n_codes
            + [by_rows(self.width, self.rank)]
            + [by_cols(self.rows, self.width)] * n_far
            + extra_specs,
            outs,
            out_shapes,
            scratch,
            self.flops(2 + self.local),
            (grads, weights, *codes, u, *far_parts, *extra),
            name,
        )

    def hidden_grad(self, cotangent, w_out, backs, u_out, far_parts, slope, v_in, w_in):
        def finish(g, j, total, refs):
            s_ref, v_ref, w_ref, pg_ref, code_ref = refs[:5]
            outs = refs[5 : 5 + self.far]
            sum_ref = refs[-1]
            grad = (total * s_ref[:, self.cut(j)]).astype(BF16)
            pg_ref[:, self.cut(j)] = grad
            for k in range(self.far):
                outs[k][:, self.cut(j)] = dot_nt(grad, w_ref[j, 1 + self.local + k]).astype(BF16)
            part = dot_nt(grad, v_ref[:, self.cut(j)])
            if j == 0:
                sum_ref[...] = jnp.where(g == 0, part, sum_ref[...] + part)
            else:
                sum_ref[...] += part
            if j == self.group - 1:
                code_ref[...] = sum_ref[...].astype(BF16)

        weight_spec = pl.BlockSpec(
            (self.group, self.slots, self.blk, self.blk), lambda g: (g, 0, 0, 0)
        )
        got = self.backward(
            cotangent,
            w_out,
            backs,
            u_out,
            far_parts,
            finish,
            [by_cols(self.rows, self.width), whole((self.rows, self.rank))]
            + [by_cols(self.rows, self.width)] * self.far,
            [shape_of((self.rows, self.cols)), shape_of((self.rows, self.rank))]
            + [shape_of((self.rows, self.cols))] * self.far,
            [slope, v_in, w_in],
            [by_cols(self.rows, self.width), by_cols(self.rank, self.width), weight_spec],
            [pltpu.VMEM((self.rows, self.rank), F32)],
            "hidden_grad",
        )
        return got[0], got[1], got[2:]

    def input_grad(self, pre_grad, w_in, backs, u_in, far_parts):
        def finish(g, j, total, refs):
            refs[0][:, self.cut(j)] = total.astype(BF16)

        return self.backward(
            pre_grad,
            w_in,
            backs,
            u_in,
            far_parts,
            finish,
            [by_cols(self.rows, self.width)],
            [shape_of((self.rows, self.cols))],
            [],
            [],
            [],
            "input_grad",
        )[0]

    def weight_grads(self, acts, far_acts, grads, codes, backs, spot, n_tok, n_sub):
        n_far, n_codes = len(far_acts), len(codes)
        height = self.blk // (n_tok * n_sub)
        parts = self.slots + 2

        def body(spot_ref, a_ref, *refs):
            far_refs, refs = refs[:n_far], refs[n_far:]
            g_ref, refs = refs[0], refs[1:]
            code_refs, refs = refs[:n_codes], refs[n_codes:]
            back_refs, refs = refs[:n_codes], refs[n_codes:]
            outs, hold = refs[:n_sub], refs[n_sub]
            g = pl.program_id(0)
            code = sum(ref[...].astype(F32) for ref in code_refs).astype(BF16)
            back = sum(ref[...].astype(F32) for ref in back_refs).astype(BF16)
            for j in range(self.group):
                stacked = jnp.concatenate(
                    [self.columns(a_ref, self.place(g, j, k)) for k in range(1 + self.local)]
                    + [ref[:, self.cut(j)] for ref in far_refs]
                    + [code],
                    axis=1,
                )
                grad = g_ref[:, self.cut(j)]
                hold[: parts - 1] = dot_tn(stacked, grad).reshape(parts - 1, self.blk, self.blk)
                hold[parts - 1] = dot_tn(back, self.columns(a_ref, self.place(g, j, 0)))
                for m in range(n_tok):
                    for h in range(n_sub):
                        first = ((spot_ref[0] ^ m) * n_sub + (spot_ref[1] ^ h)) * height
                        outs[h][m, j] = hold[
                            :, pl.ds(pl.multiple_of(first, height), height), :
                        ].astype(BF16)

        shape = (n_tok, self.blocks, parts, height, self.blk)
        spec = pl.BlockSpec(
            (n_tok, self.group, parts, height, self.blk), lambda g: (0, g, 0, 0, 0)
        )
        args = (spot, acts, *far_acts, grads, *codes, *backs)
        return call(
            body,
            (self.steps,),
            [pl.BlockSpec(memory_space=pltpu.SMEM), whole(acts.shape)]
            + [by_cols(self.rows, self.width)] * (n_far + 1)
            + [whole((self.rows, self.rank))] * (2 * n_codes),
            [spec] * n_sub,
            [shape_of(shape)] * n_sub,
            [pltpu.VMEM((parts, self.blk, self.blk), F32)],
            self.flops(parts),
            args,
            "weight_grads",
        )

    def core_sums(self, kept, got):
        n_tok, blocks, parts, height, blk = kept.shape
        others = n_tok - 1

        def body(*refs):
            ins, outs = refs[: len(refs) - others], refs[len(refs) - others :]
            for m in range(others):
                outs[m][...] = sum(ref[1 + m].astype(F32) for ref in ins).astype(BF16)

        spec_in = pl.BlockSpec((n_tok, self.group, parts, height, blk), lambda g: (0, g, 0, 0, 0))
        spec_out = pl.BlockSpec((self.group, parts, height, blk), lambda g: (g, 0, 0, 0))
        return call(
            body,
            (self.steps,),
            [spec_in] * (1 + len(got)),
            [spec_out] * others,
            [shape_of((blocks, parts, height, blk))] * others,
            [],
            0,
            (kept, *got),
            "core_sums",
        )

    def last_sums(self, kept, got, arrived):
        n_tok, blocks, parts, height, blk = kept.shape
        n_near, n_far = 1 + len(got), len(arrived)

        def body(*refs):
            near, far, (w_ref, v_ref, u_ref) = refs[:n_near], refs[n_near:-3], refs[-3:]
            for j in range(self.group):
                total = sum(ref[0, j].astype(F32) for ref in near)
                for ref in far:
                    total = total + ref[j].astype(F32)
                w_ref[j] = total[: parts - 2]
                v_ref[:, self.cut(j)] = total[parts - 2]
                u_ref[self.cut(j), :] = total[parts - 1].T

        spec_near = pl.BlockSpec((1, self.group, parts, height, blk), lambda g: (0, g, 0, 0, 0))
        spec_far = pl.BlockSpec((self.group, parts, height, blk), lambda g: (g, 0, 0, 0))
        return call(
            body,
            (self.steps,),
            [spec_near] * n_near + [spec_far] * n_far,
            [
                pl.BlockSpec((self.group, parts - 2, height, blk), lambda g: (g, 0, 0, 0)),
                by_cols(height, self.width),
                by_rows(self.width, height),
            ],
            [
                shape_of((blocks, parts - 2, height, blk), F32),
                shape_of((height, self.cols), F32),
                shape_of((self.cols, height), F32),
            ],
            [],
            0,
            (kept, *got, *arrived),
            "last_sums",
        )


def shards(inputs, cotangent, w_in, w_out, u_in, v_in, u_out, v_out):
    layer = Layer(inputs, w_in)
    n_feat, n_tok, n_sub = (lax.axis_size(name) for name in ("feat", "tok", "sub"))
    spot = jnp.stack([lax.axis_index("tok"), lax.axis_index("sub")]).astype(jnp.int32)

    def to_partners(values):
        return [exchange(value, "feat", 1 << k) for k, value in enumerate(values)]

    def to_all(part):
        return [part] + [exchange(part, "feat", mask) for mask in range(1, n_feat)]

    def summed(parts):
        kept = parts[0]
        got = [exchange(parts[h], "sub", h) for h in range(1, n_sub)]
        sums = layer.core_sums(kept, got) if n_tok > 1 else []
        arrived = [exchange(value, "tok", 1 + m) for m, value in enumerate(sums)]
        return layer.last_sums(kept, got, arrived)

    far_inputs = to_partners([inputs] * layer.far)
    code_part, back_part = layer.first_codes(inputs, cotangent, u_in, v_out)
    codes_in, backs_out = to_all(code_part), to_all(back_part)
    far_cot = to_partners(layer.far_products(cotangent, w_out, far_inputs[:1]))

    act, slope, code_part = layer.hidden(inputs, far_inputs, w_in, codes_in, v_in, u_out)
    far_acts = to_partners([act] * layer.far)
    codes_out = to_all(code_part)

    pre_grad, back_part, products = layer.hidden_grad(
        cotangent, w_out, backs_out, u_out, far_cot, slope, v_in, w_in
    )
    far_pre = to_partners(products)
    backs_in = to_all(back_part)

    parts_in = layer.weight_grads(
        inputs, far_inputs, pre_grad, codes_in, backs_in, spot, n_tok, n_sub
    )
    grad_w_in, grad_v_in, grad_u_in = summed(parts_in)

    output = layer.result(act, far_acts, w_out, codes_out, v_out)
    parts_out = layer.weight_grads(
        act, far_acts, cotangent, codes_out, backs_out, spot, n_tok, n_sub
    )
    grad_w_out, grad_v_out, grad_u_out = summed(parts_out)
    in_grad = layer.input_grad(pre_grad, w_in, backs_in, u_in, far_pre)
    return (output, in_grad, grad_w_in, grad_w_out, grad_u_in, grad_v_in, grad_u_out, grad_v_out)


def solution(mesh):
    placed = (
        P(("group", "tok", "sub"), "feat"),
        P(("group", "tok", "sub"), "feat"),
        P("feat", None, None, None),
        P("feat", None, None, None),
        P("feat", None),
        P(None, "feat"),
        P("feat", None),
        P(None, "feat"),
    )
    return jax.shard_map(
        shards,
        mesh=mesh,
        in_specs=placed,
        out_specs=(
            P(("group", "tok", "sub"), "feat"),
            P(("group", "tok", "sub"), "feat"),
            P(("group", "feat"), None, ("tok", "sub"), None),
            P(("group", "feat"), None, ("tok", "sub"), None),
            P(("group", "feat"), ("tok", "sub")),
            P(("group", "tok", "sub"), "feat"),
            P(("group", "feat"), ("tok", "sub")),
            P(("group", "tok", "sub"), "feat"),
        ),
        check_vma=False,
    )
```

```python
import math

import jax
import jax.numpy as jnp
from jax import lax
from jax.experimental import pallas as pl
from jax.experimental.pallas import tpu as pltpu
from jax.sharding import PartitionSpec as P

F32 = jnp.float32
BF16 = jnp.bfloat16
VMEM_LIMIT = 60 * 1024 * 1024


def exchange(value, axis, mask):
    pairs = [(source, source ^ mask) for source in range(lax.axis_size(axis))]
    return lax.ppermute(value, axis, pairs)


def gelu_parts(pre):
    factor = math.sqrt(2.0 / math.pi)
    square = pre * pre
    tangent = jnp.tanh(factor * (pre + 0.044715 * square * pre))
    active = 0.5 * pre * (1.0 + tangent)
    slope = 0.5 * (1.0 + tangent) + 0.5 * pre * (1.0 - tangent * tangent) * factor * (
        1.0 + 3.0 * 0.044715 * square
    )
    return (active, slope)


def dot(left, right):
    return jnp.dot(left, right, preferred_element_type=F32)


def dot_nt(left, right):
    return lax.dot_general(left, right, (((1,), (1,)), ((), ())), preferred_element_type=F32)


def dot_tn(left, right):
    return lax.dot_general(left, right, (((0,), (0,)), ((), ())), preferred_element_type=F32)


def whole(shape):
    return pl.BlockSpec(shape, lambda g: (0,) * len(shape))


def by_cols(rows, width):
    return pl.BlockSpec((rows, width), lambda g: (0, g))


def by_rows(height, cols):
    return pl.BlockSpec((height, cols), lambda g: (g, 0))


def shape_of(shape, dtype=BF16):
    return jax.ShapeDtypeStruct(shape, dtype)


def call(body, grid, ins, outs, out_shapes, scratch, flops, args, name, after=()):
    moved = sum(a.size * a.dtype.itemsize for a in args) + sum(
        math.prod(s.shape) * s.dtype.itemsize for s in out_shapes
    )
    count = len(args)

    def kernel(*refs):
        body(*refs[:count], *refs[count + len(after) :])

    return pl.pallas_call(
        kernel,
        grid=grid,
        in_specs=list(ins) + [pl.BlockSpec(memory_space=pl.ANY)] * len(after),
        out_specs=outs,
        out_shape=out_shapes,
        scratch_shapes=scratch,
        compiler_params=pltpu.CompilerParams(vmem_limit_bytes=VMEM_LIMIT),
        cost_estimate=pl.CostEstimate(flops=flops, bytes_accessed=moved, transcendentals=0),
        name=name,
    )(*args, *after)


def pin(values, *after):
    def body(*refs):
        del refs

    count = len(values)
    anywhere = pl.BlockSpec(memory_space=pl.ANY)
    return pl.pallas_call(
        body,
        in_specs=[anywhere] * (count + len(after)),
        out_specs=[anywhere] * count,
        out_shape=[shape_of(value.shape, value.dtype) for value in values],
        input_output_aliases={i: i for i in range(count)},
        cost_estimate=pl.CostEstimate(flops=0, bytes_accessed=0, transcendentals=0),
        name="pin",
    )(*values, *after)


class Layer:
    def __init__(self, inputs, weights):
        self.rows, self.cols = inputs.shape
        self.blocks, self.slots, self.blk, _ = weights.shape
        self.local = self.blocks.bit_length() - 1
        self.far = self.slots - 1 - self.local
        self.group = min(4, self.blocks)
        self.steps = self.blocks // self.group
        self.width = self.group * self.blk
        self.rank = self.blk

    def cut(self, j):
        return slice(j * self.blk, (j + 1) * self.blk)

    def place(self, g, j, k):
        if k == 0:
            return g * self.group + j
        mask = 1 << (k - 1)
        if mask < self.group:
            return g * self.group + (j ^ mask)
        return (g ^ (mask // self.group)) * self.group + j

    def columns(self, ref, block):
        return ref[:, pl.ds(pl.multiple_of(block * self.blk, self.blk), self.blk)]

    def code_specs(self, codes):
        return [
            pl.BlockSpec((self.rows, self.rank), lambda g, at=at: (at, 0)) for _, at in codes
        ]

    def code_of(self, refs):
        return sum(ref[...].astype(F32) for ref in refs).astype(BF16) if refs else None

    def flops(self, per_block):
        return 2 * self.rows * self.blk * self.blk * self.blocks * per_block

    def first_codes(self, inputs, cotangent, u_in, v_out, after=()):
        def body(x_ref, c_ref, u_ref, v_ref, code_ref):
            code_ref[: self.rows] = dot(x_ref[...], u_ref[...]).astype(BF16)
            code_ref[self.rows :] = dot_nt(c_ref[...], v_ref[...]).astype(BF16)

        return call(
            body,
            (1,),
            [whole(inputs.shape), whole(inputs.shape), whole(u_in.shape), whole(v_out.shape)],
            [whole((2 * self.rows, self.rank))],
            [shape_of((2 * self.rows, self.rank))],
            [],
            self.flops(2),
            (inputs, cotangent, u_in, v_out),
            "first_codes",
            after,
        )[0]

    def far_products(self, grads, weights, after=()):
        def body(g_ref, w_ref, *outs):
            for j in range(self.group):
                block = g_ref[:, self.cut(j)]
                for k in range(self.far):
                    outs[k][:, self.cut(j)] = dot_nt(
                        block, w_ref[j, 1 + self.local + k]
                    ).astype(BF16)

        weight_spec = pl.BlockSpec(
            (self.group, self.slots, self.blk, self.blk), lambda g: (g, 0, 0, 0)
        )
        return call(
            body,
            (self.steps,),
            [by_cols(self.rows, self.width), weight_spec],
            [by_cols(self.rows, self.width)] * self.far,
            [shape_of((self.rows, self.cols))] * self.far,
            [],
            self.flops(self.far),
            (grads, weights),
            "far_products",
            after,
        )

    def forward(self, acts, far_acts, weights, codes, v, finish, outs, out_shapes, extra, extra_specs, scratch, name, after=()):
        n_far, n_codes, n_extra = len(far_acts), len(codes), len(extra)

        def body(a_ref, *refs):
            far_refs, refs = refs[:n_far], refs[n_far:]
            w_ref, refs = refs[0], refs[1:]
            code_refs, refs = refs[:n_codes], refs[n_codes:]
            v_ref, refs = refs[0], refs[1:]
            g = pl.program_id(0)
            code = self.code_of(code_refs)
            for j in range(self.group):
                parts = [
                    self.columns(a_ref, self.place(g, j, k)) for k in range(1 + self.local)
                ] + [ref[:, self.cut(j)] for ref in far_refs]
                stacked = jnp.concatenate(parts, axis=1)
                weight = w_ref[j].reshape(self.slots * self.blk, self.blk)
                total = dot(stacked, weight) + dot(code, v_ref[:, self.cut(j)])
                finish(g, j, total, refs)

        weight_spec = pl.BlockSpec(
            (self.group, self.slots, self.blk, self.blk), lambda g: (g, 0, 0, 0)
        )
        return call(
            body,
            (self.steps,),
            [whole(acts.shape)]
            + [by_cols(self.rows, self.width)] * n_far
            + [weight_spec]
            + self.code_specs(codes)
            + [by_cols(self.rank, self.width)]
            + extra_specs,
            outs,
            out_shapes,
            scratch,
            self.flops(self.slots + 2),
            (acts, *far_acts, weights, *(value for value, _ in codes), v, *extra),
            name,
            after,
        )

    def hidden(self, inputs, far_inputs, w_in, codes, v_in, u_out, after=()):
        def finish(g, j, pre, refs):
            u_ref, act_ref, slope_ref, code_ref, sum_ref = refs
            active, slope = gelu_parts(pre)
            act = active.astype(BF16)
            act_ref[:, self.cut(j)] = act
            slope_ref[:, self.cut(j)] = slope
            part = dot(act, u_ref[self.cut(j), :])
            if j == 0:
                sum_ref[...] = jnp.where(g == 0, part, sum_ref[...] + part)
            else:
                sum_ref[...] += part
            if j == self.group - 1:
                code_ref[...] = sum_ref[...].astype(BF16)

        return self.forward(
            inputs,
            far_inputs,
            w_in,
            codes,
            v_in,
            finish,
            [by_cols(self.rows, self.width)] * 2 + [whole((self.rows, self.rank))],
            [
                shape_of((self.rows, self.cols)),
                shape_of((self.rows, self.cols), F32),
                shape_of((self.rows, self.rank)),
            ],
            [u_out],
            [by_rows(self.width, self.rank)],
            [pltpu.VMEM((self.rows, self.rank), F32)],
            "hidden",
            after,
        )

    def result(self, act, far_acts, w_out, codes, v_out, after=()):
        def finish(g, j, total, refs):
            refs[0][:, self.cut(j)] = total.astype(BF16)

        return self.forward(
            act,
            far_acts,
            w_out,
            codes,
            v_out,
            finish,
            [by_cols(self.rows, self.width)],
            [shape_of((self.rows, self.cols))],
            [],
            [],
            [],
            "result",
            after,
        )[0]

    def backward(self, grads, weights, codes, u, far_parts, finish, outs, out_shapes, extra, extra_specs, scratch, name, after=()):
        n_far, n_codes, n_extra = len(far_parts), len(codes), len(extra)

        def body(g_ref, w_ref, *refs):
            code_refs, refs = refs[:n_codes], refs[n_codes:]
            u_ref, refs = refs[0], refs[1:]
            far_refs, refs = refs[:n_far], refs[n_far:]
            g = pl.program_id(0)
            code = self.code_of(code_refs)
            for j in range(self.group):
                places = [self.place(g, j, k) for k in range(1 + self.local)]
                stacked = jnp.concatenate(
                    [self.columns(g_ref, place) for place in places] + [code], axis=1
                )
                weight = jnp.concatenate(
                    [w_ref[place, k] for k, place in enumerate(places)] + [u_ref[self.cut(j), :]],
                    axis=1,
                )
                total = dot_nt(stacked, weight)
                for ref in far_refs:
                    total = total + ref[:, self.cut(j)].astype(F32)
                finish(g, j, total, refs)

        return call(
            body,
            (self.steps,),
            [whole(grads.shape), whole(weights.shape)]
            + self.code_specs(codes)
            + [by_rows(self.width, self.rank)]
            + [by_cols(self.rows, self.width)] * n_far
            + extra_specs,
            outs,
            out_shapes,
            scratch,
            self.flops(2 + self.local),
            (grads, weights, *(value for value, _ in codes), u, *far_parts, *extra),
            name,
            after,
        )

    def hidden_grad(self, cotangent, w_out, backs, u_out, far_parts, slope, v_in, w_in, code_part, after=()):
        def finish(g, j, total, refs):
            s_ref, v_ref, w_ref, c_ref, pg_ref, code_ref = refs[:6]
            outs = refs[6 : 6 + self.far]
            sum_ref = refs[-1]
            grad = (total * s_ref[:, self.cut(j)]).astype(BF16)
            pg_ref[:, self.cut(j)] = grad
            for k in range(self.far):
                outs[k][:, self.cut(j)] = dot_nt(grad, w_ref[j, 1 + self.local + k]).astype(BF16)
            part = dot_nt(grad, v_ref[:, self.cut(j)])
            if j == 0:
                sum_ref[...] = jnp.where(g == 0, part, sum_ref[...] + part)
            else:
                sum_ref[...] += part
            if j == self.group - 1:
                code_ref[: self.rows] = c_ref[...]
                code_ref[self.rows :] = sum_ref[...].astype(BF16)

        weight_spec = pl.BlockSpec(
            (self.group, self.slots, self.blk, self.blk), lambda g: (g, 0, 0, 0)
        )
        got = self.backward(
            cotangent,
            w_out,
            backs,
            u_out,
            far_parts,
            finish,
            [by_cols(self.rows, self.width), whole((2 * self.rows, self.rank))]
            + [by_cols(self.rows, self.width)] * self.far,
            [shape_of((self.rows, self.cols)), shape_of((2 * self.rows, self.rank))]
            + [shape_of((self.rows, self.cols))] * self.far,
            [slope, v_in, w_in, code_part],
            [
                by_cols(self.rows, self.width),
                by_cols(self.rank, self.width),
                weight_spec,
                whole(code_part.shape),
            ],
            [pltpu.VMEM((self.rows, self.rank), F32)],
            "hidden_grad",
            after,
        )
        return got[0], got[1], got[2:]

    def input_grad(self, pre_grad, w_in, backs, u_in, after=()):
        def finish(g, j, total, refs):
            refs[0][:, self.cut(j)] = total

        return self.backward(
            pre_grad,
            w_in,
            backs,
            u_in,
            [],
            finish,
            [by_cols(self.rows, self.width)],
            [shape_of((self.rows, self.cols), F32)],
            [],
            [],
            [],
            "input_grad",
            after,
        )[0]

    def weight_grads(self, cuts, grads, acts=None, far_acts=(), codes=(), backs=(), u_acts=None, after=()):
        spot, n_tok, n_sub = cuts
        height = self.blk // (n_tok * n_sub)
        n_local = 0 if acts is None else 1 + self.local
        n_stack = n_local + len(far_acts) + (1 if codes else 0)
        parts = n_stack + (1 if backs else 0)

        def body(spot_ref, *refs):
            refs = list(refs)
            take = lambda count: [refs.pop(0) for _ in range(count)]
            (g_ref,) = take(1)
            acts_ref = take(0 if acts is None else 1)
            far_refs = take(len(far_acts))
            code_refs, back_refs = take(len(codes)), take(len(backs))
            u_ref = take(1 if backs else 0)
            outs, hold = refs[:n_sub], refs[n_sub]
            g = pl.program_id(0)
            code, back = self.code_of(code_refs), self.code_of(back_refs)
            for j in range(self.group):
                pieces = [self.columns(acts_ref[0], self.place(g, j, k)) for k in range(n_local)]
                pieces += [ref[:, self.cut(j)] for ref in far_refs]
                pieces += [code] if codes else []
                grad = g_ref[:, self.cut(j)]
                hold[:n_stack] = dot_tn(jnp.concatenate(pieces, axis=1), grad).reshape(
                    n_stack, self.blk, self.blk
                )
                if backs:
                    hold[n_stack] = dot_tn(back, u_ref[0][:, self.cut(j)])
                for m in range(n_tok):
                    for h in range(n_sub):
                        first = ((spot_ref[0] ^ m) * n_sub + (spot_ref[1] ^ h)) * height
                        outs[h][m, j] = hold[
                            :, pl.ds(pl.multiple_of(first, height), height), :
                        ].astype(BF16)

        shape = (n_tok, self.blocks, parts, height, self.blk)
        spec = pl.BlockSpec(
            (n_tok, self.group, parts, height, self.blk), lambda g: (0, g, 0, 0, 0)
        )
        cols = by_cols(self.rows, self.width)
        return call(
            body,
            (self.steps,),
            [pl.BlockSpec(memory_space=pltpu.SMEM), cols]
            + ([] if acts is None else [whole(acts.shape)])
            + [cols] * len(far_acts)
            + self.code_specs(codes)
            + self.code_specs(backs)
            + ([cols] if backs else []),
            [spec] * n_sub,
            [shape_of(shape)] * n_sub,
            [pltpu.VMEM((parts, self.blk, self.blk), F32)],
            self.flops(parts),
            [spot, grads]
            + ([] if acts is None else [acts])
            + list(far_acts)
            + [value for value, _ in (*codes, *backs)]
            + ([u_acts] if backs else []),
            "weight_grads",
            after,
        )

    def core_sums(self, kept, got, after=()):
        n_tok, blocks, parts, height, blk = kept.shape
        others = n_tok - 1

        def body(*refs):
            ins, outs = refs[: len(refs) - others], refs[len(refs) - others :]
            for m in range(others):
                outs[m][...] = sum(ref[1 + m].astype(F32) for ref in ins).astype(BF16)

        spec_in = pl.BlockSpec((n_tok, self.group, parts, height, blk), lambda g: (0, g, 0, 0, 0))
        spec_out = pl.BlockSpec((self.group, parts, height, blk), lambda g: (g, 0, 0, 0))
        return call(
            body,
            (self.steps,),
            [spec_in] * (1 + len(got)),
            [spec_out] * others,
            [shape_of((blocks, parts, height, blk))] * others,
            [],
            0,
            (kept, *got),
            "core_sums",
            after,
        )

    def last_sums(self, sums, targets, after=()):
        sizes = [1 + len(got) + len(arrived) for _, got, arrived in sums]
        near = [1 + len(got) for _, got, _ in sums]
        height, blk = sums[0][0].shape[3:]

        def body(*refs):
            ins, outs = refs[: sum(sizes)], refs[sum(sizes) :]
            for j in range(self.group):
                totals, at = [], 0
                for size, count in zip(sizes, near):
                    totals.append(
                        sum(
                            (ref[0, j] if i < count else ref[j]).astype(F32)
                            for i, ref in enumerate(ins[at : at + size])
                        )
                    )
                    at += size
                for target, ref in zip(targets, outs):
                    if isinstance(target, list):
                        to = 0
                        for which, first, count in target:
                            ref[j, to : to + count] = totals[which][first : first + count]
                            to += count
                    else:
                        ref[:, self.cut(j)] = totals[target[0]][target[1]]

        ins, args = [], []
        for kept, got, arrived in sums:
            n_tok, blocks, parts = kept.shape[:3]
            spec_near = pl.BlockSpec(
                (1, self.group, parts, height, blk), lambda g: (0, g, 0, 0, 0)
            )
            spec_far = pl.BlockSpec((self.group, parts, height, blk), lambda g: (g, 0, 0, 0))
            ins += [spec_near] * (1 + len(got)) + [spec_far] * len(arrived)
            args += [kept, *got, *arrived]
        outs, shapes = [], []
        for target in targets:
            if isinstance(target, list):
                count = sum(c for _, _, c in target)
                outs.append(pl.BlockSpec((self.group, count, height, blk), lambda g: (g, 0, 0, 0)))
                shapes.append(shape_of((self.blocks, count, height, blk), F32))
            else:
                outs.append(by_cols(height, self.width))
                shapes.append(shape_of((height, self.cols), F32))
        return call(body, (self.steps,), ins, outs, shapes, [], 0, args, "last_sums", after)

    def final(self, local, far_parts, after=()):
        def body(l_ref, *refs):
            total = l_ref[...]
            for ref in refs[:-1]:
                total = total + ref[...].astype(F32)
            refs[-1][...] = total.astype(BF16)

        cols = by_cols(self.rows, self.width)
        return call(
            body,
            (self.steps,),
            [cols] * (1 + len(far_parts)),
            [cols],
            [shape_of((self.rows, self.cols))],
            [],
            0,
            (local, *far_parts),
            "final",
            after,
        )[0]


def shards(inputs, cotangent, w_in, w_out, u_in, v_in, u_out, v_out):
    layer = Layer(inputs, w_in)
    n_feat, n_tok, n_sub = (lax.axis_size(name) for name in ("feat", "tok", "sub"))
    spot = jnp.stack([lax.axis_index("tok"), lax.axis_index("sub")]).astype(jnp.int32)
    cuts = (spot, n_tok, n_sub)

    def to_partners(values):
        return [exchange(value, "feat", 1 << k) for k, value in enumerate(values)]

    def to_all(part):
        return [part] + [exchange(part, "feat", mask) for mask in range(1, n_feat)]

    def by_levels(part):
        parts = [part]
        for level in range(n_feat.bit_length() - 1):
            if level:
                part = (parts[0].astype(F32) + parts[1].astype(F32)).astype(BF16)
            parts = [part, exchange(part, "feat", 1 << level)]
        return parts

    def halves(parts):
        return [(value, 0) for value in parts], [(value, 1) for value in parts]

    def block(work, *args):
        shapes = jax.eval_shape(work, *args)
        empty = lambda *_: jax.tree.map(lambda x: jnp.zeros(x.shape, x.dtype), shapes)
        return lax.cond(lax.axis_index("feat") < n_feat, work, empty, *args)

    def summed(parts):
        kept = parts[0]
        got = [exchange(parts[h], "sub", h) for h in range(1, n_sub)]
        sums = layer.core_sums(kept, got) if n_tok > 1 else []
        return kept, got, [exchange(value, "tok", 1 + m) for m, value in enumerate(sums)]

    def start_step(inputs, cotangent, w_out, u_in, v_out):
        products = layer.far_products(cotangent, w_out)
        return products, to_all(layer.first_codes(inputs, cotangent, u_in, v_out))

    def hidden_step(inputs, cotangent, w_in, v_in, u_out, far_inputs, first):
        codes, backs = halves(first)
        act, slope, code = layer.hidden(inputs, far_inputs, w_in, codes, v_in, u_out)
        parts = layer.weight_grads(cuts, cotangent, acts=act, backs=backs, u_acts=act)
        return act, slope, code, summed(parts)

    def grad_step(
        inputs, cotangent, w_in, w_out, v_in, u_out, far_inputs, far_cot, slope, code, first
    ):
        codes, backs = halves(first)
        pre_grad, code, products = layer.hidden_grad(
            cotangent, w_out, backs, u_out, far_cot, slope, v_in, w_in, code
        )
        parts = layer.weight_grads(cuts, pre_grad, acts=inputs, far_acts=far_inputs, codes=codes)
        return pre_grad, by_levels(code), products, summed(parts)

    def last_step(inputs, cotangent, w_in, w_out, v_out, u_in, act, far_acts, last, pre_grad):
        codes, backs = halves(last)
        parts = layer.weight_grads(
            cuts, cotangent, far_acts=far_acts, codes=codes, backs=backs, u_acts=inputs
        )
        output = layer.result(act, far_acts, w_out, codes, v_out, after=parts[:1])
        return output, layer.input_grad(pre_grad, w_in, backs, u_in), summed(parts)

    far_inputs = to_partners([inputs] * layer.far)
    products, first = block(start_step, inputs, cotangent, w_out, u_in, v_out)
    far_cot = to_partners(products)
    act, slope, code, sums_early = block(
        hidden_step, inputs, cotangent, w_in, v_in, u_out, far_inputs, first
    )
    far_acts = to_partners([act] * layer.far)
    pre_grad, last, products, sums_in = block(
        grad_step,
        inputs, cotangent, w_in, w_out, v_in, u_out, far_inputs, far_cot, slope, code, first,
    )
    far_pre = to_partners(pin(products, *far_acts))
    output, local_grad, sums_late = block(
        last_step, inputs, cotangent, w_in, w_out, v_out, u_in, act, far_acts, last, pre_grad
    )
    near, slots = 1 + layer.local, layer.slots
    grad_w_in, grad_v_in = layer.last_sums(
        [sums_in], [[(0, 0, slots)], (0, slots)], after=[output]
    )
    grad_w_out, grad_u_out, grad_v_out, grad_u_in = layer.last_sums(
        [sums_early, sums_late],
        [[(0, 0, near), (1, 0, layer.far)], (0, near), (1, layer.far), (1, layer.far + 1)],
    )
    total = local_grad
    for value in far_pre:
        total = total + value.astype(F32)
    in_grad = total.astype(BF16)
    return (
        output,
        in_grad,
        grad_w_in,
        grad_w_out,
        grad_u_in.T,
        grad_v_in,
        grad_u_out.T,
        grad_v_out,
    )


def solution(mesh):
    placed = (
        P(("group", "tok", "sub"), "feat"),
        P(("group", "tok", "sub"), "feat"),
        P("feat", None, None, None),
        P("feat", None, None, None),
        P("feat", None),
        P(None, "feat"),
        P("feat", None),
        P(None, "feat"),
    )
    return jax.shard_map(
        shards,
        mesh=mesh,
        in_specs=placed,
        out_specs=(
            P(("group", "tok", "sub"), "feat"),
            P(("group", "tok", "sub"), "feat"),
            P(("group", "feat"), None, ("tok", "sub"), None),
            P(("group", "feat"), None, ("tok", "sub"), None),
            P(("group", "feat"), ("tok", "sub")),
            P(("group", "tok", "sub"), "feat"),
            P(("group", "feat"), ("tok", "sub")),
            P(("group", "tok", "sub"), "feat"),
        ),
        check_vma=False,
    )
```

```python
import math

import jax
import jax.numpy as jnp
from jax import lax
from jax.experimental import pallas as pl
from jax.experimental.pallas import tpu as pltpu
from jax.sharding import PartitionSpec as P

F32 = jnp.float32
BF16 = jnp.bfloat16
VMEM_LIMIT = 60 * 1024 * 1024


def exchange(value, axis, mask):
    pairs = [(source, source ^ mask) for source in range(lax.axis_size(axis))]
    return lax.ppermute(value, axis, pairs)


def gelu_parts(pre):
    factor = math.sqrt(2.0 / math.pi)
    square = pre * pre
    tangent = jnp.tanh(factor * (pre + 0.044715 * square * pre))
    active = 0.5 * pre * (1.0 + tangent)
    slope = 0.5 * (1.0 + tangent) + 0.5 * pre * (1.0 - tangent * tangent) * factor * (
        1.0 + 3.0 * 0.044715 * square
    )
    return (active, slope)


def dot(left, right):
    return jnp.dot(left, right, preferred_element_type=F32)


def dot_nt(left, right):
    return lax.dot_general(left, right, (((1,), (1,)), ((), ())), preferred_element_type=F32)


def dot_tn(left, right):
    return lax.dot_general(left, right, (((0,), (0,)), ((), ())), preferred_element_type=F32)


def whole(shape):
    return pl.BlockSpec(shape, lambda g: (0,) * len(shape))


def by_cols(rows, width):
    return pl.BlockSpec((rows, width), lambda g: (0, g))


def by_rows(height, cols):
    return pl.BlockSpec((height, cols), lambda g: (g, 0))


def shape_of(shape, dtype=BF16):
    return jax.ShapeDtypeStruct(shape, dtype)


def call(body, grid, ins, outs, out_shapes, scratch, flops, args, name, after=()):
    moved = sum(a.size * a.dtype.itemsize for a in args) + sum(
        math.prod(s.shape) * s.dtype.itemsize for s in out_shapes
    )
    count = len(args)

    def kernel(*refs):
        body(*refs[:count], *refs[count + len(after) :])

    return pl.pallas_call(
        kernel,
        grid=grid,
        in_specs=list(ins) + [pl.BlockSpec(memory_space=pl.ANY)] * len(after),
        out_specs=outs,
        out_shape=out_shapes,
        scratch_shapes=scratch,
        compiler_params=pltpu.CompilerParams(vmem_limit_bytes=VMEM_LIMIT),
        cost_estimate=pl.CostEstimate(flops=flops, bytes_accessed=moved, transcendentals=0),
        name=name,
    )(*args, *after)


def pin(values, *after):
    def body(*refs):
        del refs

    count = len(values)
    anywhere = pl.BlockSpec(memory_space=pl.ANY)
    return pl.pallas_call(
        body,
        in_specs=[anywhere] * (count + len(after)),
        out_specs=[anywhere] * count,
        out_shape=[shape_of(value.shape, value.dtype) for value in values],
        input_output_aliases={i: i for i in range(count)},
        cost_estimate=pl.CostEstimate(flops=0, bytes_accessed=0, transcendentals=0),
        name="pin",
    )(*values, *after)


class Layer:
    def __init__(self, inputs, weights):
        self.rows, self.cols = inputs.shape
        self.blocks, self.slots, self.blk, _ = weights.shape
        self.local = self.blocks.bit_length() - 1
        self.far = self.slots - 1 - self.local
        self.group = min(4, self.blocks)
        self.steps = self.blocks // self.group
        self.width = self.group * self.blk
        self.rank = self.blk

    def cut(self, j):
        return slice(j * self.blk, (j + 1) * self.blk)

    def place(self, g, j, k):
        if k == 0:
            return g * self.group + j
        mask = 1 << (k - 1)
        if mask < self.group:
            return g * self.group + (j ^ mask)
        return (g ^ (mask // self.group)) * self.group + j

    def columns(self, ref, block):
        return ref[:, pl.ds(pl.multiple_of(block * self.blk, self.blk), self.blk)]

    def code_specs(self, codes):
        return [
            pl.BlockSpec((self.rows, self.rank), lambda g, at=at: (at, 0)) for _, at in codes
        ]

    def code_of(self, refs):
        return sum(ref[...].astype(F32) for ref in refs).astype(BF16) if refs else None

    def flops(self, per_block):
        return 2 * self.rows * self.blk * self.blk * self.blocks * per_block

    def first_codes(self, inputs, cotangent, u_in, v_out, after=()):
        def body(x_ref, c_ref, u_ref, v_ref, code_ref):
            code_ref[: self.rows] = dot(x_ref[...], u_ref[...]).astype(BF16)
            code_ref[self.rows :] = dot_nt(c_ref[...], v_ref[...]).astype(BF16)

        return call(
            body,
            (1,),
            [whole(inputs.shape), whole(inputs.shape), whole(u_in.shape), whole(v_out.shape)],
            [whole((2 * self.rows, self.rank))],
            [shape_of((2 * self.rows, self.rank))],
            [],
            self.flops(2),
            (inputs, cotangent, u_in, v_out),
            "first_codes",
            after,
        )[0]

    def far_products(self, grads, weights, after=()):
        def body(g_ref, w_ref, *outs):
            for j in range(self.group):
                block = g_ref[:, self.cut(j)]
                for k in range(self.far):
                    outs[k][:, self.cut(j)] = dot_nt(
                        block, w_ref[j, 1 + self.local + k]
                    ).astype(BF16)

        weight_spec = pl.BlockSpec(
            (self.group, self.slots, self.blk, self.blk), lambda g: (g, 0, 0, 0)
        )
        return call(
            body,
            (self.steps,),
            [by_cols(self.rows, self.width), weight_spec],
            [by_cols(self.rows, self.width)] * self.far,
            [shape_of((self.rows, self.cols))] * self.far,
            [],
            self.flops(self.far),
            (grads, weights),
            "far_products",
            after,
        )

    def forward(self, acts, far_acts, weights, codes, v, finish, outs, out_shapes, extra, extra_specs, scratch, name, after=()):
        n_far, n_codes, n_extra = len(far_acts), len(codes), len(extra)

        def body(a_ref, *refs):
            far_refs, refs = refs[:n_far], refs[n_far:]
            w_ref, refs = refs[0], refs[1:]
            code_refs, refs = refs[:n_codes], refs[n_codes:]
            v_ref, refs = refs[0], refs[1:]
            g = pl.program_id(0)
            code = self.code_of(code_refs)
            for j in range(self.group):
                parts = [
                    self.columns(a_ref, self.place(g, j, k)) for k in range(1 + self.local)
                ] + [ref[:, self.cut(j)] for ref in far_refs]
                stacked = jnp.concatenate(parts, axis=1)
                weight = w_ref[j].reshape(self.slots * self.blk, self.blk)
                total = dot(stacked, weight) + dot(code, v_ref[:, self.cut(j)])
                finish(g, j, total, refs)

        weight_spec = pl.BlockSpec(
            (self.group, self.slots, self.blk, self.blk), lambda g: (g, 0, 0, 0)
        )
        return call(
            body,
            (self.steps,),
            [whole(acts.shape)]
            + [by_cols(self.rows, self.width)] * n_far
            + [weight_spec]
            + self.code_specs(codes)
            + [by_cols(self.rank, self.width)]
            + extra_specs,
            outs,
            out_shapes,
            scratch,
            self.flops(self.slots + 2),
            (acts, *far_acts, weights, *(value for value, _ in codes), v, *extra),
            name,
            after,
        )

    def hidden(self, inputs, far_inputs, w_in, codes, v_in, u_out, after=()):
        def finish(g, j, pre, refs):
            u_ref, act_ref, slope_ref, code_ref, sum_ref = refs
            active, slope = gelu_parts(pre)
            act = active.astype(BF16)
            act_ref[:, self.cut(j)] = act
            slope_ref[:, self.cut(j)] = slope
            part = dot(act, u_ref[self.cut(j), :])
            if j == 0:
                sum_ref[...] = jnp.where(g == 0, part, sum_ref[...] + part)
            else:
                sum_ref[...] += part
            if j == self.group - 1:
                code_ref[...] = sum_ref[...].astype(BF16)

        return self.forward(
            inputs,
            far_inputs,
            w_in,
            codes,
            v_in,
            finish,
            [by_cols(self.rows, self.width)] * 2 + [whole((self.rows, self.rank))],
            [
                shape_of((self.rows, self.cols)),
                shape_of((self.rows, self.cols), F32),
                shape_of((self.rows, self.rank)),
            ],
            [u_out],
            [by_rows(self.width, self.rank)],
            [pltpu.VMEM((self.rows, self.rank), F32)],
            "hidden",
            after,
        )

    def result(self, act, far_acts, w_out, codes, v_out, after=()):
        def finish(g, j, total, refs):
            refs[0][:, self.cut(j)] = total.astype(BF16)

        return self.forward(
            act,
            far_acts,
            w_out,
            codes,
            v_out,
            finish,
            [by_cols(self.rows, self.width)],
            [shape_of((self.rows, self.cols))],
            [],
            [],
            [],
            "result",
            after,
        )[0]

    def backward(self, grads, weights, codes, u, far_parts, finish, outs, out_shapes, extra, extra_specs, scratch, name, after=()):
        n_far, n_codes, n_extra = len(far_parts), len(codes), len(extra)

        def body(g_ref, w_ref, *refs):
            code_refs, refs = refs[:n_codes], refs[n_codes:]
            u_ref, refs = refs[0], refs[1:]
            far_refs, refs = refs[:n_far], refs[n_far:]
            g = pl.program_id(0)
            code = self.code_of(code_refs)
            for j in range(self.group):
                places = [self.place(g, j, k) for k in range(1 + self.local)]
                stacked = jnp.concatenate(
                    [self.columns(g_ref, place) for place in places] + [code], axis=1
                )
                weight = jnp.concatenate(
                    [w_ref[place, k] for k, place in enumerate(places)] + [u_ref[self.cut(j), :]],
                    axis=1,
                )
                total = dot_nt(stacked, weight)
                for ref in far_refs:
                    total = total + ref[:, self.cut(j)].astype(F32)
                finish(g, j, total, refs)

        return call(
            body,
            (self.steps,),
            [whole(grads.shape), whole(weights.shape)]
            + self.code_specs(codes)
            + [by_rows(self.width, self.rank)]
            + [by_cols(self.rows, self.width)] * n_far
            + extra_specs,
            outs,
            out_shapes,
            scratch,
            self.flops(2 + self.local),
            (grads, weights, *(value for value, _ in codes), u, *far_parts, *extra),
            name,
            after,
        )

    def hidden_grad(self, cotangent, w_out, backs, u_out, far_parts, slope, v_in, w_in, code_part, after=()):
        def finish(g, j, total, refs):
            s_ref, v_ref, w_ref, c_ref, pg_ref, code_ref = refs[:6]
            outs = refs[6 : 6 + self.far]
            sum_ref = refs[-1]
            grad = (total * s_ref[:, self.cut(j)]).astype(BF16)
            pg_ref[:, self.cut(j)] = grad
            for k in range(self.far):
                outs[k][:, self.cut(j)] = dot_nt(grad, w_ref[j, 1 + self.local + k]).astype(BF16)
            part = dot_nt(grad, v_ref[:, self.cut(j)])
            if j == 0:
                sum_ref[...] = jnp.where(g == 0, part, sum_ref[...] + part)
            else:
                sum_ref[...] += part
            if j == self.group - 1:
                code_ref[: self.rows] = c_ref[...]
                code_ref[self.rows :] = sum_ref[...].astype(BF16)

        weight_spec = pl.BlockSpec(
            (self.group, self.slots, self.blk, self.blk), lambda g: (g, 0, 0, 0)
        )
        got = self.backward(
            cotangent,
            w_out,
            backs,
            u_out,
            far_parts,
            finish,
            [by_cols(self.rows, self.width), whole((2 * self.rows, self.rank))]
            + [by_cols(self.rows, self.width)] * self.far,
            [shape_of((self.rows, self.cols)), shape_of((2 * self.rows, self.rank))]
            + [shape_of((self.rows, self.cols))] * self.far,
            [slope, v_in, w_in, code_part],
            [
                by_cols(self.rows, self.width),
                by_cols(self.rank, self.width),
                weight_spec,
                whole(code_part.shape),
            ],
            [pltpu.VMEM((self.rows, self.rank), F32)],
            "hidden_grad",
            after,
        )
        return got[0], got[1], got[2:]

    def input_grad(self, pre_grad, w_in, backs, u_in, after=()):
        def finish(g, j, total, refs):
            refs[0][:, self.cut(j)] = total

        return self.backward(
            pre_grad,
            w_in,
            backs,
            u_in,
            [],
            finish,
            [by_cols(self.rows, self.width)],
            [shape_of((self.rows, self.cols), F32)],
            [],
            [],
            [],
            "input_grad",
            after,
        )[0]

    def weight_grads(self, cuts, grads, acts=None, far_acts=(), codes=(), backs=(), u_acts=None, after=()):
        spot, n_tok, n_sub = cuts
        height = self.blk // (n_tok * n_sub)
        n_local = 0 if acts is None else 1 + self.local
        n_stack = n_local + len(far_acts) + (1 if codes else 0)
        parts = n_stack + (1 if backs else 0)

        def body(spot_ref, *refs):
            refs = list(refs)
            take = lambda count: [refs.pop(0) for _ in range(count)]
            (g_ref,) = take(1)
            acts_ref = take(0 if acts is None else 1)
            far_refs = take(len(far_acts))
            code_refs, back_refs = take(len(codes)), take(len(backs))
            u_ref = take(1 if backs else 0)
            outs, hold = refs[:n_sub], refs[n_sub]
            g = pl.program_id(0)
            code, back = self.code_of(code_refs), self.code_of(back_refs)
            for j in range(self.group):
                pieces = [self.columns(acts_ref[0], self.place(g, j, k)) for k in range(n_local)]
                pieces += [ref[:, self.cut(j)] for ref in far_refs]
                pieces += [code] if codes else []
                grad = g_ref[:, self.cut(j)]
                hold[:n_stack] = dot_tn(jnp.concatenate(pieces, axis=1), grad).reshape(
                    n_stack, self.blk, self.blk
                )
                if backs:
                    hold[n_stack] = dot_tn(back, u_ref[0][:, self.cut(j)])
                for m in range(n_tok):
                    for h in range(n_sub):
                        first = ((spot_ref[0] ^ m) * n_sub + (spot_ref[1] ^ h)) * height
                        outs[h][m, j] = hold[
                            :, pl.ds(pl.multiple_of(first, height), height), :
                        ].astype(BF16)

        shape = (n_tok, self.blocks, parts, height, self.blk)
        spec = pl.BlockSpec(
            (n_tok, self.group, parts, height, self.blk), lambda g: (0, g, 0, 0, 0)
        )
        cols = by_cols(self.rows, self.width)
        return call(
            body,
            (self.steps,),
            [pl.BlockSpec(memory_space=pltpu.SMEM), cols]
            + ([] if acts is None else [whole(acts.shape)])
            + [cols] * len(far_acts)
            + self.code_specs(codes)
            + self.code_specs(backs)
            + ([cols] if backs else []),
            [spec] * n_sub,
            [shape_of(shape)] * n_sub,
            [pltpu.VMEM((parts, self.blk, self.blk), F32)],
            self.flops(parts),
            [spot, grads]
            + ([] if acts is None else [acts])
            + list(far_acts)
            + [value for value, _ in (*codes, *backs)]
            + ([u_acts] if backs else []),
            "weight_grads",
            after,
        )

    def core_sums(self, kept, got, after=()):
        n_tok, blocks, parts, height, blk = kept.shape
        others = n_tok - 1

        def body(*refs):
            ins, outs = refs[: len(refs) - others], refs[len(refs) - others :]
            for m in range(others):
                outs[m][...] = sum(ref[1 + m].astype(F32) for ref in ins).astype(BF16)

        spec_in = pl.BlockSpec((n_tok, self.group, parts, height, blk), lambda g: (0, g, 0, 0, 0))
        spec_out = pl.BlockSpec((self.group, parts, height, blk), lambda g: (g, 0, 0, 0))
        return call(
            body,
            (self.steps,),
            [spec_in] * (1 + len(got)),
            [spec_out] * others,
            [shape_of((blocks, parts, height, blk))] * others,
            [],
            0,
            (kept, *got),
            "core_sums",
            after,
        )

    def last_sums(self, sums, targets, after=()):
        sizes = [1 + len(got) + len(arrived) for _, got, arrived in sums]
        near = [1 + len(got) for _, got, _ in sums]
        height, blk = sums[0][0].shape[3:]

        def body(*refs):
            ins, outs = refs[: sum(sizes)], refs[sum(sizes) :]
            for j in range(self.group):
                totals, at = [], 0
                for size, count in zip(sizes, near):
                    totals.append(
                        sum(
                            (ref[0, j] if i < count else ref[j]).astype(F32)
                            for i, ref in enumerate(ins[at : at + size])
                        )
                    )
                    at += size
                for target, ref in zip(targets, outs):
                    if isinstance(target, list):
                        to = 0
                        for which, first, count in target:
                            ref[j, to : to + count] = totals[which][first : first + count]
                            to += count
                    else:
                        ref[:, self.cut(j)] = totals[target[0]][target[1]]

        ins, args = [], []
        for kept, got, arrived in sums:
            n_tok, blocks, parts = kept.shape[:3]
            spec_near = pl.BlockSpec(
                (1, self.group, parts, height, blk), lambda g: (0, g, 0, 0, 0)
            )
            spec_far = pl.BlockSpec((self.group, parts, height, blk), lambda g: (g, 0, 0, 0))
            ins += [spec_near] * (1 + len(got)) + [spec_far] * len(arrived)
            args += [kept, *got, *arrived]
        outs, shapes = [], []
        for target in targets:
            if isinstance(target, list):
                count = sum(c for _, _, c in target)
                outs.append(pl.BlockSpec((self.group, count, height, blk), lambda g: (g, 0, 0, 0)))
                shapes.append(shape_of((self.blocks, count, height, blk), F32))
            else:
                outs.append(by_cols(height, self.width))
                shapes.append(shape_of((height, self.cols), F32))
        return call(body, (self.steps,), ins, outs, shapes, [], 0, args, "last_sums", after)

    def final(self, local, far_parts, after=()):
        def body(l_ref, *refs):
            total = l_ref[...]
            for ref in refs[:-1]:
                total = total + ref[...].astype(F32)
            refs[-1][...] = total.astype(BF16)

        cols = by_cols(self.rows, self.width)
        return call(
            body,
            (self.steps,),
            [cols] * (1 + len(far_parts)),
            [cols],
            [shape_of((self.rows, self.cols))],
            [],
            0,
            (local, *far_parts),
            "final",
            after,
        )[0]


def shards(inputs, cotangent, w_in, w_out, u_in, v_in, u_out, v_out):
    layer = Layer(inputs, w_in)
    n_feat, n_tok, n_sub = (lax.axis_size(name) for name in ("feat", "tok", "sub"))
    spot = jnp.stack([lax.axis_index("tok"), lax.axis_index("sub")]).astype(jnp.int32)
    cuts = (spot, n_tok, n_sub)

    def to_partners(values):
        sent = [exchange(value, "feat", 1 << k) for k, value in reversed(list(enumerate(values)))]
        return sent[::-1]

    def add(parts):
        return (parts[0].astype(F32) + parts[1].astype(F32)).astype(BF16)

    def by_levels(part):
        parts = [part, exchange(part, "feat", 1)]
        for level in range(1, n_feat.bit_length() - 2):
            part = add(parts)
            parts = [part, exchange(part, "feat", 1 << level)]
        return add(parts)

    def last_level(part):
        return [part, exchange(part, "feat", n_feat // 2)]

    def halves(parts):
        return [(value, 0) for value in parts], [(value, 1) for value in parts]

    def block(work, *args):
        shapes = jax.eval_shape(work, *args)
        empty = lambda *_: jax.tree.map(lambda x: jnp.zeros(x.shape, x.dtype), shapes)
        return lax.cond(lax.axis_index("feat") < n_feat, work, empty, *args)

    def by_cores(parts):
        kept = parts[0]
        got = [exchange(parts[h], "sub", h) for h in range(1, n_sub)]
        return kept, got, list(layer.core_sums(kept, got)) if n_tok > 1 else []

    def by_chips(kept, got, sums):
        return kept, got, [exchange(value, "tok", 1 + m) for m, value in enumerate(sums)]

    def summed(parts):
        return by_chips(*by_cores(parts))

    def start_step(inputs, cotangent, w_out, u_in, v_out):
        products = layer.far_products(cotangent, w_out)
        return products, by_levels(layer.first_codes(inputs, cotangent, u_in, v_out))

    def hidden_step(inputs, cotangent, w_in, v_in, u_out, far_inputs, first):
        codes, backs = halves(first)
        act, slope, code = layer.hidden(inputs, far_inputs, w_in, codes, v_in, u_out)
        parts = layer.weight_grads(cuts, cotangent, acts=act, backs=backs, u_acts=act)
        return act, slope, code, by_cores(parts)

    def grad_step(
        inputs, cotangent, w_in, w_out, v_in, u_out, far_inputs, far_cot, slope, code, first, done
    ):
        codes, backs = halves(first)
        pre_grad, code, products = layer.hidden_grad(
            cotangent, w_out, backs, u_out, far_cot, slope, v_in, w_in, code, after=done
        )
        parts = layer.weight_grads(cuts, pre_grad, acts=inputs, far_acts=far_inputs, codes=codes)
        return pre_grad, last_level(by_levels(code)), products, summed(parts)

    def last_step(inputs, cotangent, w_in, w_out, v_out, u_in, act, far_acts, last, pre_grad):
        codes, backs = halves(last)
        parts = layer.weight_grads(
            cuts, cotangent, far_acts=far_acts, codes=codes, backs=backs, u_acts=inputs
        )
        output = layer.result(act, far_acts, w_out, codes, v_out, after=parts[:1])
        return output, layer.input_grad(pre_grad, w_in, backs, u_in), summed(parts)

    far_inputs = to_partners([inputs] * layer.far)
    products, first = block(start_step, inputs, cotangent, w_out, u_in, v_out)
    first = last_level(first)
    far_cot = to_partners(products)
    act, slope, code, sums_early = block(
        hidden_step, inputs, cotangent, w_in, v_in, u_out, far_inputs, first
    )
    far_acts = to_partners([act] * layer.far)
    sums_early = by_chips(*sums_early)
    pre_grad, last, products, sums_in = block(
        grad_step,
        inputs, cotangent, w_in, w_out, v_in, u_out, far_inputs, far_cot, slope, code, first,
        sums_early[2],
    )
    far_pre = to_partners(pin(products, *far_acts))
    output, local_grad, sums_late = block(
        last_step, inputs, cotangent, w_in, w_out, v_out, u_in, act, far_acts, last, pre_grad
    )
    near, slots = 1 + layer.local, layer.slots
    grad_w_in, grad_v_in = layer.last_sums(
        [sums_in], [[(0, 0, slots)], (0, slots)], after=[output]
    )
    grad_w_out, grad_u_out, grad_v_out, grad_u_in = layer.last_sums(
        [sums_early, sums_late],
        [[(0, 0, near), (1, 0, layer.far)], (0, near), (1, layer.far), (1, layer.far + 1)],
    )
    total = local_grad
    for value in far_pre:
        total = total + value.astype(F32)
    in_grad = total.astype(BF16)
    return (
        output,
        in_grad,
        grad_w_in,
        grad_w_out,
        grad_u_in.T,
        grad_v_in,
        grad_u_out.T,
        grad_v_out,
    )


def solution(mesh):
    placed = (
        P(("group", "tok", "sub"), "feat"),
        P(("group", "tok", "sub"), "feat"),
        P("feat", None, None, None),
        P("feat", None, None, None),
        P("feat", None),
        P(None, "feat"),
        P("feat", None),
        P(None, "feat"),
    )
    return jax.shard_map(
        shards,
        mesh=mesh,
        in_specs=placed,
        out_specs=(
            P(("group", "tok", "sub"), "feat"),
            P(("group", "tok", "sub"), "feat"),
            P(("group", "feat"), None, ("tok", "sub"), None),
            P(("group", "feat"), None, ("tok", "sub"), None),
            P(("group", "feat"), ("tok", "sub")),
            P(("group", "tok", "sub"), "feat"),
            P(("group", "feat"), ("tok", "sub")),
            P(("group", "tok", "sub"), "feat"),
        ),
        check_vma=False,
    )
```

```python
import math

import jax
import jax.numpy as jnp
from jax import lax
from jax.experimental import pallas as pl
from jax.experimental.pallas import tpu as pltpu
from jax.sharding import PartitionSpec as P

F32 = jnp.float32
BF16 = jnp.bfloat16
VMEM_LIMIT = 60 * 1024 * 1024


def exchange(value, axis, mask):
    pairs = [(source, source ^ mask) for source in range(lax.axis_size(axis))]
    return lax.ppermute(value, axis, pairs)


def gelu_parts(pre):
    factor = math.sqrt(2.0 / math.pi)
    square = pre * pre
    tangent = jnp.tanh(factor * (pre + 0.044715 * square * pre))
    active = 0.5 * pre * (1.0 + tangent)
    slope = 0.5 * (1.0 + tangent) + 0.5 * pre * (1.0 - tangent * tangent) * factor * (
        1.0 + 3.0 * 0.044715 * square
    )
    return (active, slope)


def dot(left, right):
    return jnp.dot(left, right, preferred_element_type=F32)


def dot_nt(left, right):
    return lax.dot_general(left, right, (((1,), (1,)), ((), ())), preferred_element_type=F32)


def dot_tn(left, right):
    return lax.dot_general(left, right, (((0,), (0,)), ((), ())), preferred_element_type=F32)


def whole(shape):
    return pl.BlockSpec(shape, lambda g: (0,) * len(shape))


def by_cols(rows, width):
    return pl.BlockSpec((rows, width), lambda g: (0, g))


def by_rows(height, cols):
    return pl.BlockSpec((height, cols), lambda g: (g, 0))


def shape_of(shape, dtype=BF16):
    return jax.ShapeDtypeStruct(shape, dtype)


def call(body, grid, ins, outs, out_shapes, scratch, flops, args, name, after=()):
    moved = sum(a.size * a.dtype.itemsize for a in args) + sum(
        math.prod(s.shape) * s.dtype.itemsize for s in out_shapes
    )
    count = len(args)

    def kernel(*refs):
        body(*refs[:count], *refs[count + len(after) :])

    return pl.pallas_call(
        kernel,
        grid=grid,
        in_specs=list(ins) + [pl.BlockSpec(memory_space=pl.ANY)] * len(after),
        out_specs=outs,
        out_shape=out_shapes,
        scratch_shapes=scratch,
        compiler_params=pltpu.CompilerParams(
            vmem_limit_bytes=VMEM_LIMIT if name != "input_grad" else 24 * 1024 * 1024
        ),
        cost_estimate=pl.CostEstimate(flops=flops, bytes_accessed=moved, transcendentals=0),
        name=name,
    )(*args, *after)


def pin(values, *after):
    def body(*refs):
        del refs

    count = len(values)
    anywhere = pl.BlockSpec(memory_space=pl.ANY)
    return pl.pallas_call(
        body,
        in_specs=[anywhere] * (count + len(after)),
        out_specs=[anywhere] * count,
        out_shape=[shape_of(value.shape, value.dtype) for value in values],
        input_output_aliases={i: i for i in range(count)},
        cost_estimate=pl.CostEstimate(flops=0, bytes_accessed=0, transcendentals=0),
        name="pin",
    )(*values, *after)


class Layer:
    def __init__(self, inputs, weights):
        self.rows, self.cols = inputs.shape
        self.blocks, self.slots, self.blk, _ = weights.shape
        self.local = self.blocks.bit_length() - 1
        self.far = self.slots - 1 - self.local
        self.group = min(4, self.blocks)
        self.steps = self.blocks // self.group
        self.width = self.group * self.blk
        self.rank = self.blk

    def cut(self, j):
        return slice(j * self.blk, (j + 1) * self.blk)

    def place(self, g, j, k):
        if k == 0:
            return g * self.group + j
        mask = 1 << (k - 1)
        if mask < self.group:
            return g * self.group + (j ^ mask)
        return (g ^ (mask // self.group)) * self.group + j

    def columns(self, ref, block):
        return ref[:, pl.ds(pl.multiple_of(block * self.blk, self.blk), self.blk)]

    def code_specs(self, codes):
        return [
            pl.BlockSpec((self.rows, self.rank), lambda g, at=at: (at, 0)) for _, at in codes
        ]

    def code_of(self, refs):
        return sum(ref[...].astype(F32) for ref in refs).astype(BF16) if refs else None

    def flops(self, per_block):
        return 2 * self.rows * self.blk * self.blk * self.blocks * per_block

    def first_codes(self, inputs, cotangent, u_in, v_out, after=()):
        def body(x_ref, c_ref, u_ref, v_ref, code_ref):
            code_ref[: self.rows] = dot(x_ref[...], u_ref[...]).astype(BF16)
            code_ref[self.rows :] = dot_nt(c_ref[...], v_ref[...]).astype(BF16)

        return call(
            body,
            (1,),
            [whole(inputs.shape), whole(inputs.shape), whole(u_in.shape), whole(v_out.shape)],
            [whole((2 * self.rows, self.rank))],
            [shape_of((2 * self.rows, self.rank))],
            [],
            self.flops(2),
            (inputs, cotangent, u_in, v_out),
            "first_codes",
            after,
        )[0]

    def far_products(self, grads, weights, after=()):
        def body(g_ref, w_ref, *outs):
            for j in range(self.group):
                block = g_ref[:, self.cut(j)]
                for k in range(self.far):
                    outs[k][:, self.cut(j)] = dot_nt(
                        block, w_ref[j, 1 + self.local + k]
                    ).astype(BF16)

        weight_spec = pl.BlockSpec(
            (self.group, self.slots, self.blk, self.blk), lambda g: (g, 0, 0, 0)
        )
        return call(
            body,
            (self.steps,),
            [by_cols(self.rows, self.width), weight_spec],
            [by_cols(self.rows, self.width)] * self.far,
            [shape_of((self.rows, self.cols))] * self.far,
            [],
            self.flops(self.far),
            (grads, weights),
            "far_products",
            after,
        )

    def forward(self, acts, far_acts, weights, codes, v, finish, outs, out_shapes, extra, extra_specs, scratch, name, after=()):
        n_far, n_codes, n_extra = len(far_acts), len(codes), len(extra)

        def body(a_ref, *refs):
            far_refs, refs = refs[:n_far], refs[n_far:]
            w_ref, refs = refs[0], refs[1:]
            code_refs, refs = refs[:n_codes], refs[n_codes:]
            v_ref, refs = refs[0], refs[1:]
            g = pl.program_id(0)
            code = self.code_of(code_refs)
            for j in range(self.group):
                parts = [
                    self.columns(a_ref, self.place(g, j, k)) for k in range(1 + self.local)
                ] + [ref[:, self.cut(j)] for ref in far_refs]
                stacked = jnp.concatenate(parts, axis=1)
                weight = w_ref[j].reshape(self.slots * self.blk, self.blk)
                total = dot(stacked, weight) + dot(code, v_ref[:, self.cut(j)])
                finish(g, j, total, refs)

        weight_spec = pl.BlockSpec(
            (self.group, self.slots, self.blk, self.blk), lambda g: (g, 0, 0, 0)
        )
        return call(
            body,
            (self.steps,),
            [whole(acts.shape)]
            + [by_cols(self.rows, self.width)] * n_far
            + [weight_spec]
            + self.code_specs(codes)
            + [by_cols(self.rank, self.width)]
            + extra_specs,
            outs,
            out_shapes,
            scratch,
            self.flops(self.slots + 2),
            (acts, *far_acts, weights, *(value for value, _ in codes), v, *extra),
            name,
            after,
        )

    def hidden(self, inputs, far_inputs, w_in, codes, v_in, u_out, after=()):
        def finish(g, j, pre, refs):
            u_ref, act_ref, slope_ref, code_ref, sum_ref = refs
            active, slope = gelu_parts(pre)
            act = active.astype(BF16)
            act_ref[:, self.cut(j)] = act
            slope_ref[:, self.cut(j)] = slope
            part = dot(act, u_ref[self.cut(j), :])
            if j == 0:
                sum_ref[...] = jnp.where(g == 0, part, sum_ref[...] + part)
            else:
                sum_ref[...] += part
            if j == self.group - 1:
                code_ref[...] = sum_ref[...].astype(BF16)

        return self.forward(
            inputs,
            far_inputs,
            w_in,
            codes,
            v_in,
            finish,
            [by_cols(self.rows, self.width)] * 2 + [whole((self.rows, self.rank))],
            [
                shape_of((self.rows, self.cols)),
                shape_of((self.rows, self.cols), F32),
                shape_of((self.rows, self.rank)),
            ],
            [u_out],
            [by_rows(self.width, self.rank)],
            [pltpu.VMEM((self.rows, self.rank), F32)],
            "hidden",
            after,
        )

    def result(self, act, far_acts, w_out, codes, v_out, after=()):
        def finish(g, j, total, refs):
            refs[0][:, self.cut(j)] = total.astype(BF16)

        return self.forward(
            act,
            far_acts,
            w_out,
            codes,
            v_out,
            finish,
            [by_cols(self.rows, self.width)],
            [shape_of((self.rows, self.cols))],
            [],
            [],
            [],
            "result",
            after,
        )[0]

    def backward(self, grads, weights, codes, u, far_parts, finish, outs, out_shapes, extra, extra_specs, scratch, name, after=()):
        n_far, n_codes, n_extra = len(far_parts), len(codes), len(extra)

        def body(g_ref, w_ref, *refs):
            code_refs, refs = refs[:n_codes], refs[n_codes:]
            u_ref, refs = refs[0], refs[1:]
            far_refs, refs = refs[:n_far], refs[n_far:]
            g = pl.program_id(0)
            code = self.code_of(code_refs)
            for j in range(self.group):
                places = [self.place(g, j, k) for k in range(1 + self.local)]
                stacked = jnp.concatenate(
                    [self.columns(g_ref, place) for place in places] + [code], axis=1
                )
                weight = jnp.concatenate(
                    [w_ref[place, k] for k, place in enumerate(places)] + [u_ref[self.cut(j), :]],
                    axis=1,
                )
                total = dot_nt(stacked, weight)
                for ref in far_refs:
                    total = total + ref[:, self.cut(j)].astype(F32)
                finish(g, j, total, refs)

        return call(
            body,
            (self.steps,),
            [whole(grads.shape), whole(weights.shape)]
            + self.code_specs(codes)
            + [by_rows(self.width, self.rank)]
            + [by_cols(self.rows, self.width)] * n_far
            + extra_specs,
            outs,
            out_shapes,
            scratch,
            self.flops(2 + self.local),
            (grads, weights, *(value for value, _ in codes), u, *far_parts, *extra),
            name,
            after,
        )

    def hidden_grad(self, cotangent, w_out, backs, u_out, far_parts, slope, v_in, w_in, code_part, cut, after=()):
        def finish(g, j, total, refs):
            s_ref, v_ref, w_ref, c_ref, pg_ref, code_ref = refs[:6]
            outs = refs[6 : 6 + 2 * self.far]
            sum_ref = refs[-1]
            grad = (total * s_ref[:, self.cut(j)]).astype(BF16)
            pg_ref[:, self.cut(j)] = grad
            for k in range(self.far):
                part = dot_nt(grad, w_ref[j, 1 + self.local + k]).astype(BF16)
                outs[k][:, self.cut(j)] = part[:cut]
                outs[self.far + k][:, self.cut(j)] = part[cut:]
            part = dot_nt(grad, v_ref[:, self.cut(j)])
            if j == 0:
                sum_ref[...] = jnp.where(g == 0, part, sum_ref[...] + part)
            else:
                sum_ref[...] += part
            if j == self.group - 1:
                code_ref[: self.rows] = c_ref[...]
                code_ref[self.rows :] = sum_ref[...].astype(BF16)

        weight_spec = pl.BlockSpec(
            (self.group, self.slots, self.blk, self.blk), lambda g: (g, 0, 0, 0)
        )
        got = self.backward(
            cotangent,
            w_out,
            backs,
            u_out,
            far_parts,
            finish,
            [by_cols(self.rows, self.width), whole((2 * self.rows, self.rank))]
            + [by_cols(cut, self.width)] * self.far
            + [by_cols(self.rows - cut, self.width)] * self.far,
            [shape_of((self.rows, self.cols)), shape_of((2 * self.rows, self.rank))]
            + [shape_of((cut, self.cols))] * self.far
            + [shape_of((self.rows - cut, self.cols))] * self.far,
            [slope, v_in, w_in, code_part],
            [
                by_cols(self.rows, self.width),
                by_cols(self.rank, self.width),
                weight_spec,
                whole(code_part.shape),
            ],
            [pltpu.VMEM((self.rows, self.rank), F32)],
            "hidden_grad",
            after,
        )
        return got[0], got[1], (got[2 : 2 + self.far], got[2 + self.far :])

    def input_grad(self, pre_grad, w_in, backs, u_in, after=()):
        def finish(g, j, total, refs):
            refs[0][:, self.cut(j)] = total

        return self.backward(
            pre_grad,
            w_in,
            backs,
            u_in,
            [],
            finish,
            [by_cols(self.rows, self.width)],
            [shape_of((self.rows, self.cols), F32)],
            [],
            [],
            [],
            "input_grad",
            after,
        )[0]

    def weight_grads(self, cuts, grads, acts=None, far_acts=(), codes=(), backs=(), u_acts=None, after=()):
        spot, n_tok, n_sub = cuts
        height = self.blk // (n_tok * n_sub)
        n_local = 0 if acts is None else 1 + self.local
        n_stack = n_local + len(far_acts) + (1 if codes else 0)
        parts = n_stack + (1 if backs else 0)

        def body(spot_ref, *refs):
            refs = list(refs)
            take = lambda count: [refs.pop(0) for _ in range(count)]
            (g_ref,) = take(1)
            acts_ref = take(0 if acts is None else 1)
            far_refs = take(len(far_acts))
            code_refs, back_refs = take(len(codes)), take(len(backs))
            u_ref = take(1 if backs else 0)
            outs, hold = refs[:n_sub], refs[n_sub]
            g = pl.program_id(0)
            code, back = self.code_of(code_refs), self.code_of(back_refs)
            for j in range(self.group):
                pieces = [self.columns(acts_ref[0], self.place(g, j, k)) for k in range(n_local)]
                pieces += [ref[:, self.cut(j)] for ref in far_refs]
                pieces += [code] if codes else []
                grad = g_ref[:, self.cut(j)]
                hold[:n_stack] = dot_tn(jnp.concatenate(pieces, axis=1), grad).reshape(
                    n_stack, self.blk, self.blk
                )
                if backs:
                    hold[n_stack] = dot_tn(back, u_ref[0][:, self.cut(j)])
                for m in range(n_tok):
                    for h in range(n_sub):
                        first = ((spot_ref[0] ^ m) * n_sub + (spot_ref[1] ^ h)) * height
                        outs[h][m, j] = hold[
                            :, pl.ds(pl.multiple_of(first, height), height), :
                        ].astype(BF16)

        shape = (n_tok, self.blocks, parts, height, self.blk)
        spec = pl.BlockSpec(
            (n_tok, self.group, parts, height, self.blk), lambda g: (0, g, 0, 0, 0)
        )
        cols = by_cols(self.rows, self.width)
        return call(
            body,
            (self.steps,),
            [pl.BlockSpec(memory_space=pltpu.SMEM), cols]
            + ([] if acts is None else [whole(acts.shape)])
            + [cols] * len(far_acts)
            + self.code_specs(codes)
            + self.code_specs(backs)
            + ([cols] if backs else []),
            [spec] * n_sub,
            [shape_of(shape)] * n_sub,
            [pltpu.VMEM((parts, self.blk, self.blk), F32)],
            self.flops(parts),
            [spot, grads]
            + ([] if acts is None else [acts])
            + list(far_acts)
            + [value for value, _ in (*codes, *backs)]
            + ([u_acts] if backs else []),
            "weight_grads",
            after,
        )

    def core_sums(self, kept, got, after=()):
        n_tok, blocks, parts, height, blk = kept.shape
        others = n_tok - 1

        def body(*refs):
            ins, outs = refs[: len(refs) - others], refs[len(refs) - others :]
            for m in range(others):
                outs[m][...] = sum(ref[1 + m].astype(F32) for ref in ins).astype(BF16)

        spec_in = pl.BlockSpec((n_tok, self.group, parts, height, blk), lambda g: (0, g, 0, 0, 0))
        spec_out = pl.BlockSpec((self.group, parts, height, blk), lambda g: (g, 0, 0, 0))
        return call(
            body,
            (self.steps,),
            [spec_in] * (1 + len(got)),
            [spec_out] * others,
            [shape_of((blocks, parts, height, blk))] * others,
            [],
            0,
            (kept, *got),
            "core_sums",
            after,
        )

    def last_sums(self, sums, targets, after=()):
        sizes = [1 + len(got) + len(arrived) for _, got, arrived in sums]
        near = [1 + len(got) for _, got, _ in sums]
        height, blk = sums[0][0].shape[3:]

        def body(*refs):
            ins, outs = refs[: sum(sizes)], refs[sum(sizes) :]
            for j in range(self.group):
                totals, at = [], 0
                for size, count in zip(sizes, near):
                    totals.append(
                        sum(
                            (ref[0, j] if i < count else ref[j]).astype(F32)
                            for i, ref in enumerate(ins[at : at + size])
                        )
                    )
                    at += size
                for target, ref in zip(targets, outs):
                    if isinstance(target, list):
                        to = 0
                        for which, first, count in target:
                            ref[j, to : to + count] = totals[which][first : first + count]
                            to += count
                    else:
                        ref[:, self.cut(j)] = totals[target[0]][target[1]]

        ins, args = [], []
        for kept, got, arrived in sums:
            n_tok, blocks, parts = kept.shape[:3]
            spec_near = pl.BlockSpec(
                (1, self.group, parts, height, blk), lambda g: (0, g, 0, 0, 0)
            )
            spec_far = pl.BlockSpec((self.group, parts, height, blk), lambda g: (g, 0, 0, 0))
            ins += [spec_near] * (1 + len(got)) + [spec_far] * len(arrived)
            args += [kept, *got, *arrived]
        outs, shapes = [], []
        for target in targets:
            if isinstance(target, list):
                count = sum(c for _, _, c in target)
                outs.append(pl.BlockSpec((self.group, count, height, blk), lambda g: (g, 0, 0, 0)))
                shapes.append(shape_of((self.blocks, count, height, blk), F32))
            else:
                outs.append(by_cols(height, self.width))
                shapes.append(shape_of((height, self.cols), F32))
        return call(body, (self.steps,), ins, outs, shapes, [], 0, args, "last_sums", after)

    def final(self, local, far_parts, first, total=None):
        height = far_parts[0].shape[0]
        count = 0 if total is None else 1

        def body(*refs):
            refs = refs[count:]
            value = refs[0][...]
            for ref in refs[1:-1]:
                value = value + ref[...].astype(F32)
            refs[-1][...] = value.astype(BF16)

        rows = pl.BlockSpec((height, self.width), lambda g: (first // height, g))
        return pl.pallas_call(
            body,
            grid=(self.steps,),
            in_specs=[pl.BlockSpec(memory_space=pl.ANY)] * count
            + [rows]
            + [by_cols(height, self.width)] * len(far_parts),
            out_specs=rows,
            out_shape=shape_of((self.rows, self.cols)),
            input_output_aliases={0: 0} if count else {},
            compiler_params=pltpu.CompilerParams(vmem_limit_bytes=24 * 1024 * 1024),
            name="final",
        )(*([total] if count else []), local, *far_parts)


def shards(inputs, cotangent, w_in, w_out, u_in, v_in, u_out, v_out):
    layer = Layer(inputs, w_in)
    n_feat, n_tok, n_sub = (lax.axis_size(name) for name in ("feat", "tok", "sub"))
    spot = jnp.stack([lax.axis_index("tok"), lax.axis_index("sub")]).astype(jnp.int32)
    cuts = (spot, n_tok, n_sub)

    def to_partners(values):
        sent = [exchange(value, "feat", 1 << k) for k, value in reversed(list(enumerate(values)))]
        return sent[::-1]

    def add(parts):
        return (parts[0].astype(F32) + parts[1].astype(F32)).astype(BF16)

    def by_levels(part):
        parts = [part, exchange(part, "feat", 1)]
        for level in range(1, n_feat.bit_length() - 2):
            part = add(parts)
            parts = [part, exchange(part, "feat", 1 << level)]
        return add(parts)

    def last_level(part):
        return [part, exchange(part, "feat", n_feat // 2)]

    def halves(parts):
        return [(value, 0) for value in parts], [(value, 1) for value in parts]

    def block(work, *args):
        shapes = jax.eval_shape(work, *args)
        empty = lambda *_: jax.tree.map(lambda x: jnp.zeros(x.shape, x.dtype), shapes)
        return lax.cond(lax.axis_index("feat") < n_feat, work, empty, *args)

    def by_cores(parts):
        kept = parts[0]
        got = [exchange(parts[h], "sub", h) for h in range(1, n_sub)]
        return kept, got, list(layer.core_sums(kept, got)) if n_tok > 1 else []

    def by_chips(kept, got, sums):
        return kept, got, [exchange(value, "tok", 1 + m) for m, value in enumerate(sums)]

    def summed(parts):
        return by_chips(*by_cores(parts))

    cut = layer.rows * 3 // 4

    def start_step(inputs, cotangent, w_out, u_in, v_out):
        products = layer.far_products(cotangent, w_out)
        return products, by_levels(layer.first_codes(inputs, cotangent, u_in, v_out))

    def hidden_step(inputs, cotangent, w_in, v_in, u_out, far_inputs, first):
        codes, backs = halves(first)
        act, slope, code = layer.hidden(inputs, far_inputs, w_in, codes, v_in, u_out)
        parts = layer.weight_grads(cuts, cotangent, acts=act, backs=backs, u_acts=act)
        return act, slope, code, by_cores(parts)

    def grad_step(
        inputs, cotangent, w_in, w_out, v_in, u_out, far_inputs, far_cot, slope, code, first, done
    ):
        codes, backs = halves(first)
        pre_grad, code, products = layer.hidden_grad(
            cotangent, w_out, backs, u_out, far_cot, slope, v_in, w_in, code, cut, after=done
        )
        parts = layer.weight_grads(cuts, pre_grad, acts=inputs, far_acts=far_inputs, codes=codes)
        return pre_grad, last_level(by_levels(code)), products, summed(parts)

    def last_step(inputs, cotangent, w_out, v_out, act, far_acts, last):
        codes, backs = halves(last)
        parts = layer.weight_grads(
            cuts, cotangent, far_acts=far_acts, codes=codes, backs=backs, u_acts=inputs
        )
        output = layer.result(act, far_acts, w_out, codes, v_out, after=parts[:1])
        return output, summed(parts)

    far_inputs = to_partners([inputs] * layer.far)
    products, first = block(start_step, inputs, cotangent, w_out, u_in, v_out)
    first = last_level(first)
    far_cot = to_partners(products)
    act, slope, code, sums_early = block(
        hidden_step, inputs, cotangent, w_in, v_in, u_out, far_inputs, first
    )
    far_acts = to_partners([act] * layer.far)
    sums_early = by_chips(*sums_early)
    pre_grad, last, products, sums_in = block(
        grad_step,
        inputs, cotangent, w_in, w_out, v_in, u_out, far_inputs, far_cot, slope, code, first,
        sums_early[2],
    )
    ready = pin(products[0], *far_acts)
    far_pre = to_partners(ready)
    far_rest = to_partners(pin(products[1], *ready))
    output, sums_late = block(
        last_step, inputs, cotangent, w_out, v_out, act, far_acts, last
    )
    near, slots = 1 + layer.local, layer.slots
    grad_w_in, grad_v_in = layer.last_sums(
        [sums_in], [[(0, 0, slots)], (0, slots)], after=[output]
    )
    grad_w_out, grad_u_out, grad_v_out, grad_u_in = layer.last_sums(
        [sums_early, sums_late],
        [[(0, 0, near), (1, 0, layer.far)], (0, near), (1, layer.far), (1, layer.far + 1)],
    )
    local_grad = layer.input_grad(pre_grad, w_in, halves(last)[1], u_in, after=[grad_v_out])
    in_grad = layer.final(local_grad, far_rest, cut, layer.final(local_grad, far_pre, 0))
    return (
        output,
        in_grad,
        grad_w_in,
        grad_w_out,
        grad_u_in.T,
        grad_v_in,
        grad_u_out.T,
        grad_v_out,
    )


def solution(mesh):
    placed = (
        P(("group", "tok", "sub"), "feat"),
        P(("group", "tok", "sub"), "feat"),
        P("feat", None, None, None),
        P("feat", None, None, None),
        P("feat", None),
        P(None, "feat"),
        P("feat", None),
        P(None, "feat"),
    )
    return jax.shard_map(
        shards,
        mesh=mesh,
        in_specs=placed,
        out_specs=(
            P(("group", "tok", "sub"), "feat"),
            P(("group", "tok", "sub"), "feat"),
            P(("group", "feat"), None, ("tok", "sub"), None),
            P(("group", "feat"), None, ("tok", "sub"), None),
            P(("group", "feat"), ("tok", "sub")),
            P(("group", "tok", "sub"), "feat"),
            P(("group", "feat"), ("tok", "sub")),
            P(("group", "tok", "sub"), "feat"),
        ),
        check_vma=False,
    )
```

```python
import math

import jax
import jax.numpy as jnp
from jax import lax
from jax.experimental import pallas as pl
from jax.experimental.pallas import tpu as pltpu
from jax.sharding import PartitionSpec as P

F32 = jnp.float32
BF16 = jnp.bfloat16
VMEM_LIMIT = 28 * 1024 * 1024


def exchange(value, axis, mask):
    pairs = [(source, source ^ mask) for source in range(lax.axis_size(axis))]
    return lax.ppermute(value, axis, pairs)


def gelu_parts(pre):
    factor = math.sqrt(2.0 / math.pi)
    square = pre * pre
    tangent = jnp.tanh(factor * (pre + 0.044715 * square * pre))
    active = 0.5 * pre * (1.0 + tangent)
    slope = 0.5 * (1.0 + tangent) + 0.5 * pre * (1.0 - tangent * tangent) * factor * (
        1.0 + 3.0 * 0.044715 * square
    )
    return (active, slope)


def dot(left, right):
    return jnp.dot(left, right, preferred_element_type=F32)


def dot_nt(left, right):
    return lax.dot_general(left, right, (((1,), (1,)), ((), ())), preferred_element_type=F32)


def dot_tn(left, right):
    return lax.dot_general(left, right, (((0,), (0,)), ((), ())), preferred_element_type=F32)


def whole(shape):
    return pl.BlockSpec(shape, lambda g: (0,) * len(shape))


def by_cols(rows, width):
    return pl.BlockSpec((rows, width), lambda g: (0, g))


def by_rows(height, cols):
    return pl.BlockSpec((height, cols), lambda g: (g, 0))


def shape_of(shape, dtype=BF16):
    return jax.ShapeDtypeStruct(shape, dtype)


def call(body, grid, ins, outs, out_shapes, scratch, flops, args, name, after=()):
    moved = sum(a.size * a.dtype.itemsize for a in args) + sum(
        math.prod(s.shape) * s.dtype.itemsize for s in out_shapes
    )
    count = len(args)

    def kernel(*refs):
        body(*refs[:count], *refs[count + len(after) :])

    return pl.pallas_call(
        kernel,
        grid=grid,
        in_specs=list(ins) + [pl.BlockSpec(memory_space=pl.ANY)] * len(after),
        out_specs=outs,
        out_shape=out_shapes,
        scratch_shapes=scratch,
        compiler_params=pltpu.CompilerParams(
            vmem_limit_bytes=VMEM_LIMIT if name != "input_grad" else 24 * 1024 * 1024
        ),
        cost_estimate=pl.CostEstimate(flops=flops, bytes_accessed=moved, transcendentals=0),
        name=name,
    )(*args, *after)


def pin(values, *after):
    def body(*refs):
        del refs

    count = len(values)
    anywhere = pl.BlockSpec(memory_space=pl.ANY)
    return pl.pallas_call(
        body,
        in_specs=[anywhere] * (count + len(after)),
        out_specs=[anywhere] * count,
        out_shape=[shape_of(value.shape, value.dtype) for value in values],
        input_output_aliases={i: i for i in range(count)},
        cost_estimate=pl.CostEstimate(flops=0, bytes_accessed=0, transcendentals=0),
        name="pin",
    )(*values, *after)


class Layer:
    def __init__(self, inputs, weights):
        self.rows, self.cols = inputs.shape
        self.blocks, self.slots, self.blk, _ = weights.shape
        self.local = self.blocks.bit_length() - 1
        self.far = self.slots - 1 - self.local
        self.group = min(4, self.blocks)
        self.steps = self.blocks // self.group
        self.width = self.group * self.blk
        self.rank = self.blk

    def cut(self, j):
        return slice(j * self.blk, (j + 1) * self.blk)

    def place(self, g, j, k):
        if k == 0:
            return g * self.group + j
        mask = 1 << (k - 1)
        if mask < self.group:
            return g * self.group + (j ^ mask)
        return (g ^ (mask // self.group)) * self.group + j

    def columns(self, ref, block):
        return ref[:, pl.ds(pl.multiple_of(block * self.blk, self.blk), self.blk)]

    def code_specs(self, codes):
        return [
            pl.BlockSpec((self.rows, self.rank), lambda g, at=at: (at, 0)) for _, at in codes
        ]

    def code_of(self, refs):
        return sum(ref[...].astype(F32) for ref in refs).astype(BF16) if refs else None

    def flops(self, per_block):
        return 2 * self.rows * self.blk * self.blk * self.blocks * per_block

    def first_codes(self, inputs, cotangent, u_in, v_out, after=()):
        def body(x_ref, c_ref, u_ref, v_ref, code_ref):
            code_ref[: self.rows] = dot(x_ref[...], u_ref[...]).astype(BF16)
            code_ref[self.rows :] = dot_nt(c_ref[...], v_ref[...]).astype(BF16)

        return call(
            body,
            (1,),
            [whole(inputs.shape), whole(inputs.shape), whole(u_in.shape), whole(v_out.shape)],
            [whole((2 * self.rows, self.rank))],
            [shape_of((2 * self.rows, self.rank))],
            [],
            self.flops(2),
            (inputs, cotangent, u_in, v_out),
            "first_codes",
            after,
        )[0]

    def far_products(self, grads, weights, after=()):
        def body(g_ref, w_ref, *outs):
            for j in range(self.group):
                block = g_ref[:, self.cut(j)]
                for k in range(self.far):
                    outs[k][:, self.cut(j)] = dot_nt(
                        block, w_ref[j, 1 + self.local + k]
                    ).astype(BF16)

        weight_spec = pl.BlockSpec(
            (self.group, self.slots, self.blk, self.blk), lambda g: (g, 0, 0, 0)
        )
        return call(
            body,
            (self.steps,),
            [by_cols(self.rows, self.width), weight_spec],
            [by_cols(self.rows, self.width)] * self.far,
            [shape_of((self.rows, self.cols))] * self.far,
            [],
            self.flops(self.far),
            (grads, weights),
            "far_products",
            after,
        )

    def forward(self, acts, far_acts, weights, codes, v, finish, outs, out_shapes, extra, extra_specs, scratch, name, after=()):
        n_far, n_codes, n_extra = len(far_acts), len(codes), len(extra)

        def body(a_ref, *refs):
            far_refs, refs = refs[:n_far], refs[n_far:]
            w_ref, refs = refs[0], refs[1:]
            code_refs, refs = refs[:n_codes], refs[n_codes:]
            v_ref, refs = refs[0], refs[1:]
            g = pl.program_id(0)
            code = self.code_of(code_refs)
            for j in range(self.group):
                parts = [
                    self.columns(a_ref, self.place(g, j, k)) for k in range(1 + self.local)
                ] + [ref[:, self.cut(j)] for ref in far_refs]
                stacked = jnp.concatenate(parts, axis=1)
                weight = w_ref[j].reshape(self.slots * self.blk, self.blk)
                total = dot(stacked, weight) + dot(code, v_ref[:, self.cut(j)])
                finish(g, j, total, refs)

        weight_spec = pl.BlockSpec(
            (self.group, self.slots, self.blk, self.blk), lambda g: (g, 0, 0, 0)
        )
        return call(
            body,
            (self.steps,),
            [whole(acts.shape)]
            + [by_cols(self.rows, self.width)] * n_far
            + [weight_spec]
            + self.code_specs(codes)
            + [by_cols(self.rank, self.width)]
            + extra_specs,
            outs,
            out_shapes,
            scratch,
            self.flops(self.slots + 2),
            (acts, *far_acts, weights, *(value for value, _ in codes), v, *extra),
            name,
            after,
        )

    def hidden(self, inputs, far_inputs, w_in, codes, v_in, u_out, after=()):
        def finish(g, j, pre, refs):
            u_ref, act_ref, slope_ref, code_ref, sum_ref = refs
            active, slope = gelu_parts(pre)
            act = active.astype(BF16)
            act_ref[:, self.cut(j)] = act
            slope_ref[:, self.cut(j)] = slope
            part = dot(act, u_ref[self.cut(j), :])
            if j == 0:
                sum_ref[...] = jnp.where(g == 0, part, sum_ref[...] + part)
            else:
                sum_ref[...] += part
            if j == self.group - 1:
                code_ref[...] = sum_ref[...].astype(BF16)

        return self.forward(
            inputs,
            far_inputs,
            w_in,
            codes,
            v_in,
            finish,
            [by_cols(self.rows, self.width)] * 2 + [whole((self.rows, self.rank))],
            [
                shape_of((self.rows, self.cols)),
                shape_of((self.rows, self.cols), F32),
                shape_of((self.rows, self.rank)),
            ],
            [u_out],
            [by_rows(self.width, self.rank)],
            [pltpu.VMEM((self.rows, self.rank), F32)],
            "hidden",
            after,
        )

    def result(self, act, far_acts, w_out, codes, v_out, after=()):
        def finish(g, j, total, refs):
            refs[0][:, self.cut(j)] = total.astype(BF16)

        return self.forward(
            act,
            far_acts,
            w_out,
            codes,
            v_out,
            finish,
            [by_cols(self.rows, self.width)],
            [shape_of((self.rows, self.cols))],
            [],
            [],
            [],
            "result",
            after,
        )[0]

    def backward(self, grads, weights, codes, u, far_parts, finish, outs, out_shapes, extra, extra_specs, scratch, name, after=()):
        n_far, n_codes, n_extra = len(far_parts), len(codes), len(extra)

        def body(g_ref, w_ref, *refs):
            code_refs, refs = refs[:n_codes], refs[n_codes:]
            u_ref, refs = refs[0], refs[1:]
            far_refs, refs = refs[:n_far], refs[n_far:]
            g = pl.program_id(0)
            code = self.code_of(code_refs)
            for j in range(self.group):
                places = [self.place(g, j, k) for k in range(1 + self.local)]
                stacked = jnp.concatenate(
                    [self.columns(g_ref, place) for place in places] + [code], axis=1
                )
                weight = jnp.concatenate(
                    [w_ref[place, k] for k, place in enumerate(places)] + [u_ref[self.cut(j), :]],
                    axis=1,
                )
                total = dot_nt(stacked, weight)
                for ref in far_refs:
                    total = total + ref[:, self.cut(j)].astype(F32)
                finish(g, j, total, refs)

        return call(
            body,
            (self.steps,),
            [whole(grads.shape), whole(weights.shape)]
            + self.code_specs(codes)
            + [by_rows(self.width, self.rank)]
            + [by_cols(self.rows, self.width)] * n_far
            + extra_specs,
            outs,
            out_shapes,
            scratch,
            self.flops(2 + self.local),
            (grads, weights, *(value for value, _ in codes), u, *far_parts, *extra),
            name,
            after,
        )

    def hidden_grad(self, cotangent, w_out, backs, u_out, far_parts, slope, v_in, w_in, code_part, cut, after=()):
        def finish(g, j, total, refs):
            s_ref, v_ref, w_ref, c_ref, pg_ref, code_ref = refs[:6]
            outs = refs[6 : 6 + 2 * self.far]
            sum_ref = refs[-1]
            grad = (total * s_ref[:, self.cut(j)]).astype(BF16)
            pg_ref[:, self.cut(j)] = grad
            for k in range(self.far):
                part = dot_nt(grad, w_ref[j, 1 + self.local + k]).astype(BF16)
                outs[k][:, self.cut(j)] = part[:cut]
                outs[self.far + k][:, self.cut(j)] = part[cut:]
            part = dot_nt(grad, v_ref[:, self.cut(j)])
            if j == 0:
                sum_ref[...] = jnp.where(g == 0, part, sum_ref[...] + part)
            else:
                sum_ref[...] += part
            if j == self.group - 1:
                code_ref[: self.rows] = c_ref[...]
                code_ref[self.rows :] = sum_ref[...].astype(BF16)

        weight_spec = pl.BlockSpec(
            (self.group, self.slots, self.blk, self.blk), lambda g: (g, 0, 0, 0)
        )
        got = self.backward(
            cotangent,
            w_out,
            backs,
            u_out,
            far_parts,
            finish,
            [by_cols(self.rows, self.width), whole((2 * self.rows, self.rank))]
            + [by_cols(cut, self.width)] * self.far
            + [by_cols(self.rows - cut, self.width)] * self.far,
            [shape_of((self.rows, self.cols)), shape_of((2 * self.rows, self.rank))]
            + [shape_of((cut, self.cols))] * self.far
            + [shape_of((self.rows - cut, self.cols))] * self.far,
            [slope, v_in, w_in, code_part],
            [
                by_cols(self.rows, self.width),
                by_cols(self.rank, self.width),
                weight_spec,
                whole(code_part.shape),
            ],
            [pltpu.VMEM((self.rows, self.rank), F32)],
            "hidden_grad",
            after,
        )
        return got[0], got[1], (got[2 : 2 + self.far], got[2 + self.far :])

    def input_grad(self, pre_grad, w_in, backs, u_in, after=()):
        def finish(g, j, total, refs):
            refs[0][:, self.cut(j)] = total

        return self.backward(
            pre_grad,
            w_in,
            backs,
            u_in,
            [],
            finish,
            [by_cols(self.rows, self.width)],
            [shape_of((self.rows, self.cols), F32)],
            [],
            [],
            [],
            "input_grad",
            after,
        )[0]

    def weight_grads(self, cuts, grads, acts=None, far_acts=(), codes=(), backs=(), u_acts=None, after=()):
        spot, n_tok, n_sub = cuts
        height = self.blk // (n_tok * n_sub)
        n_local = 0 if acts is None else 1 + self.local
        n_stack = n_local + len(far_acts) + (1 if codes else 0)
        parts = n_stack + (1 if backs else 0)

        def body(spot_ref, *refs):
            refs = list(refs)
            take = lambda count: [refs.pop(0) for _ in range(count)]
            (g_ref,) = take(1)
            acts_ref = take(0 if acts is None else 1)
            far_refs = take(len(far_acts))
            code_refs, back_refs = take(len(codes)), take(len(backs))
            u_ref = take(1 if backs else 0)
            outs, hold = refs[:n_sub], refs[n_sub]
            g = pl.program_id(0)
            code, back = self.code_of(code_refs), self.code_of(back_refs)
            for j in range(self.group):
                pieces = [self.columns(acts_ref[0], self.place(g, j, k)) for k in range(n_local)]
                pieces += [ref[:, self.cut(j)] for ref in far_refs]
                pieces += [code] if codes else []
                grad = g_ref[:, self.cut(j)]
                hold[:n_stack] = dot_tn(jnp.concatenate(pieces, axis=1), grad).reshape(
                    n_stack, self.blk, self.blk
                )
                if backs:
                    hold[n_stack] = dot_tn(back, u_ref[0][:, self.cut(j)])
                for m in range(n_tok):
                    for h in range(n_sub):
                        first = ((spot_ref[0] ^ m) * n_sub + (spot_ref[1] ^ h)) * height
                        outs[h][m, j] = hold[
                            :, pl.ds(pl.multiple_of(first, height), height), :
                        ].astype(BF16)

        shape = (n_tok, self.blocks, parts, height, self.blk)
        spec = pl.BlockSpec(
            (n_tok, self.group, parts, height, self.blk), lambda g: (0, g, 0, 0, 0)
        )
        cols = by_cols(self.rows, self.width)
        return call(
            body,
            (self.steps,),
            [pl.BlockSpec(memory_space=pltpu.SMEM), cols]
            + ([] if acts is None else [whole(acts.shape)])
            + [cols] * len(far_acts)
            + self.code_specs(codes)
            + self.code_specs(backs)
            + ([cols] if backs else []),
            [spec] * n_sub,
            [shape_of(shape)] * n_sub,
            [pltpu.VMEM((parts, self.blk, self.blk), F32)],
            self.flops(parts),
            [spot, grads]
            + ([] if acts is None else [acts])
            + list(far_acts)
            + [value for value, _ in (*codes, *backs)]
            + ([u_acts] if backs else []),
            "weight_grads",
            after,
        )

    def core_sums(self, kept, got, after=()):
        n_tok, blocks, parts, height, blk = kept.shape
        others = n_tok - 1

        def body(*refs):
            ins, outs = refs[: len(refs) - others], refs[len(refs) - others :]
            for m in range(others):
                outs[m][...] = sum(ref[1 + m].astype(F32) for ref in ins).astype(BF16)

        spec_in = pl.BlockSpec((n_tok, self.group, parts, height, blk), lambda g: (0, g, 0, 0, 0))
        spec_out = pl.BlockSpec((self.group, parts, height, blk), lambda g: (g, 0, 0, 0))
        return call(
            body,
            (self.steps,),
            [spec_in] * (1 + len(got)),
            [spec_out] * others,
            [shape_of((blocks, parts, height, blk))] * others,
            [],
            0,
            (kept, *got),
            "core_sums",
            after,
        )

    def last_sums(self, sums, targets, after=()):
        sizes = [1 + len(got) + len(arrived) for _, got, arrived in sums]
        near = [1 + len(got) for _, got, _ in sums]
        height, blk = sums[0][0].shape[3:]

        def body(*refs):
            ins, outs = refs[: sum(sizes)], refs[sum(sizes) :]
            for j in range(self.group):
                totals, at = [], 0
                for size, count in zip(sizes, near):
                    totals.append(
                        sum(
                            (ref[0, j] if i < count else ref[j]).astype(F32)
                            for i, ref in enumerate(ins[at : at + size])
                        )
                    )
                    at += size
                for target, ref in zip(targets, outs):
                    if isinstance(target, list):
                        to = 0
                        for which, first, count in target:
                            ref[j, to : to + count] = totals[which][first : first + count]
                            to += count
                    else:
                        ref[:, self.cut(j)] = totals[target[0]][target[1]]

        ins, args = [], []
        for kept, got, arrived in sums:
            n_tok, blocks, parts = kept.shape[:3]
            spec_near = pl.BlockSpec(
                (1, self.group, parts, height, blk), lambda g: (0, g, 0, 0, 0)
            )
            spec_far = pl.BlockSpec((self.group, parts, height, blk), lambda g: (g, 0, 0, 0))
            ins += [spec_near] * (1 + len(got)) + [spec_far] * len(arrived)
            args += [kept, *got, *arrived]
        outs, shapes = [], []
        for target in targets:
            if isinstance(target, list):
                count = sum(c for _, _, c in target)
                outs.append(pl.BlockSpec((self.group, count, height, blk), lambda g: (g, 0, 0, 0)))
                shapes.append(shape_of((self.blocks, count, height, blk), F32))
            else:
                outs.append(by_cols(height, self.width))
                shapes.append(shape_of((height, self.cols), F32))
        return call(body, (self.steps,), ins, outs, shapes, [], 0, args, "last_sums", after)

    def final(self, local, far_parts, first, total=None):
        height = far_parts[0].shape[0]
        count = 0 if total is None else 1

        def body(*refs):
            refs = refs[count:]
            value = refs[0][...]
            for ref in refs[1:-1]:
                value = value + ref[...].astype(F32)
            refs[-1][...] = value.astype(BF16)

        rows = pl.BlockSpec((height, self.width), lambda g: (first // height, g))
        return pl.pallas_call(
            body,
            grid=(self.steps,),
            in_specs=[pl.BlockSpec(memory_space=pl.ANY)] * count
            + [rows]
            + [by_cols(height, self.width)] * len(far_parts),
            out_specs=rows,
            out_shape=shape_of((self.rows, self.cols)),
            input_output_aliases={0: 0} if count else {},
            compiler_params=pltpu.CompilerParams(vmem_limit_bytes=24 * 1024 * 1024),
            name="final",
        )(*([total] if count else []), local, *far_parts)


def shards(inputs, cotangent, w_in, w_out, u_in, v_in, u_out, v_out):
    layer = Layer(inputs, w_in)
    n_feat, n_tok, n_sub = (lax.axis_size(name) for name in ("feat", "tok", "sub"))
    spot = jnp.stack([lax.axis_index("tok"), lax.axis_index("sub")]).astype(jnp.int32)
    cuts = (spot, n_tok, n_sub)

    def to_partners(values):
        sent = [exchange(value, "feat", 1 << k) for k, value in reversed(list(enumerate(values)))]
        return sent[::-1]

    def add(parts):
        return (parts[0].astype(F32) + parts[1].astype(F32)).astype(BF16)

    def by_levels(part):
        parts = [part, exchange(part, "feat", 1)]
        for level in range(1, n_feat.bit_length() - 2):
            part = add(parts)
            parts = [part, exchange(part, "feat", 1 << level)]
        return add(parts)

    def last_level(part):
        return [part, exchange(part, "feat", n_feat // 2)]

    def halves(parts):
        return [(value, 0) for value in parts], [(value, 1) for value in parts]

    def block(work, *args):
        shapes = jax.eval_shape(work, *args)
        empty = lambda *_: jax.tree.map(lambda x: jnp.zeros(x.shape, x.dtype), shapes)
        return lax.cond(lax.axis_index("feat") < n_feat, work, empty, *args)

    def by_cores(parts):
        kept = parts[0]
        got = [exchange(parts[h], "sub", h) for h in range(1, n_sub)]
        return kept, got, list(layer.core_sums(kept, got)) if n_tok > 1 else []

    def by_chips(kept, got, sums):
        return kept, got, [exchange(value, "tok", 1 + m) for m, value in enumerate(sums)]

    def summed(parts):
        return by_chips(*by_cores(parts))

    cut = layer.rows * 3 // 4

    def start_step(inputs, cotangent, w_out, u_in, v_out):
        products = layer.far_products(cotangent, w_out)
        return products, by_levels(layer.first_codes(inputs, cotangent, u_in, v_out))

    def hidden_step(inputs, cotangent, w_in, v_in, u_out, far_inputs, first):
        codes, backs = halves(first)
        act, slope, code = layer.hidden(inputs, far_inputs, w_in, codes, v_in, u_out)
        parts = layer.weight_grads(cuts, cotangent, acts=act, backs=backs, u_acts=act)
        return act, slope, code, by_cores(parts)

    def grad_step(
        inputs, cotangent, w_in, w_out, v_in, u_out, far_inputs, far_cot, slope, code, first, done
    ):
        codes, backs = halves(first)
        pre_grad, code, products = layer.hidden_grad(
            cotangent, w_out, backs, u_out, far_cot, slope, v_in, w_in, code, cut, after=done
        )
        parts = layer.weight_grads(cuts, pre_grad, acts=inputs, far_acts=far_inputs, codes=codes)
        return pre_grad, last_level(by_levels(code)), products, summed(parts)

    def last_step(inputs, cotangent, w_out, v_out, act, far_acts, last):
        codes, backs = halves(last)
        parts = layer.weight_grads(
            cuts, cotangent, far_acts=far_acts, codes=codes, backs=backs, u_acts=inputs
        )
        output = layer.result(act, far_acts, w_out, codes, v_out, after=parts[:1])
        return output, summed(parts)

    far_inputs = to_partners([inputs] * layer.far)
    products, first = block(start_step, inputs, cotangent, w_out, u_in, v_out)
    first = last_level(first)
    far_cot = to_partners(products)
    act, slope, code, sums_early = block(
        hidden_step, inputs, cotangent, w_in, v_in, u_out, far_inputs, first
    )
    far_acts = to_partners([act] * layer.far)
    sums_early = by_chips(*sums_early)
    pre_grad, last, products, sums_in = block(
        grad_step,
        inputs, cotangent, w_in, w_out, v_in, u_out, far_inputs, far_cot, slope, code, first,
        sums_early[2],
    )
    ready = pin(products[0], *far_acts)
    far_pre = to_partners(ready)
    far_rest = to_partners(pin(products[1], *ready))
    output, sums_late = block(
        last_step, inputs, cotangent, w_out, v_out, act, far_acts, last
    )
    near, slots = 1 + layer.local, layer.slots
    grad_w_in, grad_v_in = layer.last_sums(
        [sums_in], [[(0, 0, slots)], (0, slots)], after=[output]
    )
    grad_w_out, grad_u_out, grad_v_out, grad_u_in = layer.last_sums(
        [sums_early, sums_late],
        [[(0, 0, near), (1, 0, layer.far)], (0, near), (1, layer.far), (1, layer.far + 1)],
    )
    local_grad = layer.input_grad(pre_grad, w_in, halves(last)[1], u_in, after=[grad_v_out])
    in_grad = layer.final(local_grad, far_rest, cut, layer.final(local_grad, far_pre, 0))
    return (
        output,
        in_grad,
        grad_w_in,
        grad_w_out,
        grad_u_in.T,
        grad_v_in,
        grad_u_out.T,
        grad_v_out,
    )


def solution(mesh):
    placed = (
        P(("group", "tok", "sub"), "feat"),
        P(("group", "tok", "sub"), "feat"),
        P("feat", None, None, None),
        P("feat", None, None, None),
        P("feat", None),
        P(None, "feat"),
        P("feat", None),
        P(None, "feat"),
    )
    return jax.shard_map(
        shards,
        mesh=mesh,
        in_specs=placed,
        out_specs=(
            P(("group", "tok", "sub"), "feat"),
            P(("group", "tok", "sub"), "feat"),
            P(("group", "feat"), None, ("tok", "sub"), None),
            P(("group", "feat"), None, ("tok", "sub"), None),
            P(("group", "feat"), ("tok", "sub")),
            P(("group", "tok", "sub"), "feat"),
            P(("group", "feat"), ("tok", "sub")),
            P(("group", "tok", "sub"), "feat"),
        ),
        check_vma=False,
    )
```

```python
import math

import jax
import jax.numpy as jnp
from jax import lax
from jax.experimental import pallas as pl
from jax.experimental.pallas import tpu as pltpu
from jax.sharding import PartitionSpec as P

F32 = jnp.float32
BF16 = jnp.bfloat16
VMEM_LIMIT = 28 * 1024 * 1024


def exchange(value, axis, mask):
    pairs = [(source, source ^ mask) for source in range(lax.axis_size(axis))]
    return lax.ppermute(value, axis, pairs)


def gelu_parts(pre):
    factor = math.sqrt(2.0 / math.pi)
    square = pre * pre
    tangent = jnp.tanh(factor * (pre + 0.044715 * square * pre))
    active = 0.5 * pre * (1.0 + tangent)
    slope = 0.5 * (1.0 + tangent) + 0.5 * pre * (1.0 - tangent * tangent) * factor * (
        1.0 + 3.0 * 0.044715 * square
    )
    return (active, slope)


def dot(left, right):
    return jnp.dot(left, right, preferred_element_type=F32)


def dot_nt(left, right):
    return lax.dot_general(left, right, (((1,), (1,)), ((), ())), preferred_element_type=F32)


def dot_tn(left, right):
    return lax.dot_general(left, right, (((0,), (0,)), ((), ())), preferred_element_type=F32)


def whole(shape):
    return pl.BlockSpec(shape, lambda g: (0,) * len(shape))


def by_cols(rows, width):
    return pl.BlockSpec((rows, width), lambda g: (0, g))


def by_rows(height, cols):
    return pl.BlockSpec((height, cols), lambda g: (g, 0))


def shape_of(shape, dtype=BF16):
    return jax.ShapeDtypeStruct(shape, dtype)


def call(body, grid, ins, outs, out_shapes, scratch, flops, args, name, after=()):
    moved = sum(a.size * a.dtype.itemsize for a in args) + sum(
        math.prod(s.shape) * s.dtype.itemsize for s in out_shapes
    )
    count = len(args)

    def kernel(*refs):
        body(*refs[:count], *refs[count + len(after) :])

    return pl.pallas_call(
        kernel,
        grid=grid,
        in_specs=list(ins) + [pl.BlockSpec(memory_space=pl.ANY)] * len(after),
        out_specs=outs,
        out_shape=out_shapes,
        scratch_shapes=scratch,
        compiler_params=pltpu.CompilerParams(
            vmem_limit_bytes=VMEM_LIMIT if name != "input_grad" else 24 * 1024 * 1024
        ),
        cost_estimate=pl.CostEstimate(flops=flops, bytes_accessed=moved, transcendentals=0),
        name=name,
    )(*args, *after)


def pin(values, *after):
    def body(*refs):
        del refs

    count = len(values)
    anywhere = pl.BlockSpec(memory_space=pl.ANY)
    return pl.pallas_call(
        body,
        in_specs=[anywhere] * (count + len(after)),
        out_specs=[anywhere] * count,
        out_shape=[shape_of(value.shape, value.dtype) for value in values],
        input_output_aliases={i: i for i in range(count)},
        cost_estimate=pl.CostEstimate(flops=0, bytes_accessed=0, transcendentals=0),
        name="pin",
    )(*values, *after)


class Layer:
    def __init__(self, inputs, weights):
        self.rows, self.cols = inputs.shape
        self.blocks, self.slots, self.blk, _ = weights.shape
        self.local = self.blocks.bit_length() - 1
        self.far = self.slots - 1 - self.local
        self.group = min(4, self.blocks)
        self.steps = self.blocks // self.group
        self.width = self.group * self.blk
        self.rank = self.blk

    def cut(self, j):
        return slice(j * self.blk, (j + 1) * self.blk)

    def place(self, g, j, k):
        if k == 0:
            return g * self.group + j
        mask = 1 << (k - 1)
        if mask < self.group:
            return g * self.group + (j ^ mask)
        return (g ^ (mask // self.group)) * self.group + j

    def columns(self, ref, block):
        return ref[:, pl.ds(pl.multiple_of(block * self.blk, self.blk), self.blk)]

    def code_specs(self, codes):
        return [
            pl.BlockSpec((self.rows, self.rank), lambda g, at=at: (at, 0)) for _, at in codes
        ]

    def code_of(self, refs):
        return sum(ref[...].astype(F32) for ref in refs).astype(BF16) if refs else None

    def flops(self, per_block):
        return 2 * self.rows * self.blk * self.blk * self.blocks * per_block

    def first_codes(self, inputs, cotangent, u_in, v_out, after=()):
        def body(x_ref, c_ref, u_ref, v_ref, code_ref):
            code_ref[: self.rows] = dot(x_ref[...], u_ref[...]).astype(BF16)
            code_ref[self.rows :] = dot_nt(c_ref[...], v_ref[...]).astype(BF16)

        return call(
            body,
            (1,),
            [whole(inputs.shape), whole(inputs.shape), whole(u_in.shape), whole(v_out.shape)],
            [whole((2 * self.rows, self.rank))],
            [shape_of((2 * self.rows, self.rank))],
            [],
            self.flops(2),
            (inputs, cotangent, u_in, v_out),
            "first_codes",
            after,
        )[0]

    def far_products(self, grads, weights, after=()):
        def body(g_ref, w_ref, *outs):
            for j in range(self.group):
                block = g_ref[:, self.cut(j)]
                for k in range(self.far):
                    outs[k][:, self.cut(j)] = dot_nt(
                        block, w_ref[j, 1 + self.local + k]
                    ).astype(BF16)

        weight_spec = pl.BlockSpec(
            (self.group, self.slots, self.blk, self.blk), lambda g: (g, 0, 0, 0)
        )
        return call(
            body,
            (self.steps,),
            [by_cols(self.rows, self.width), weight_spec],
            [by_cols(self.rows, self.width)] * self.far,
            [shape_of((self.rows, self.cols))] * self.far,
            [],
            self.flops(self.far),
            (grads, weights),
            "far_products",
            after,
        )

    def forward(self, acts, far_acts, weights, codes, v, finish, outs, out_shapes, extra, extra_specs, scratch, name, after=()):
        n_far, n_codes, n_extra = len(far_acts), len(codes), len(extra)

        def body(a_ref, *refs):
            far_refs, refs = refs[:n_far], refs[n_far:]
            w_ref, refs = refs[0], refs[1:]
            code_refs, refs = refs[:n_codes], refs[n_codes:]
            v_ref, refs = refs[0], refs[1:]
            g = pl.program_id(0)
            code = self.code_of(code_refs)
            for j in range(self.group):
                parts = [
                    self.columns(a_ref, self.place(g, j, k)) for k in range(1 + self.local)
                ] + [ref[:, self.cut(j)] for ref in far_refs]
                stacked = jnp.concatenate(parts, axis=1)
                weight = w_ref[j].reshape(self.slots * self.blk, self.blk)
                total = dot(stacked, weight) + dot(code, v_ref[:, self.cut(j)])
                finish(g, j, total, refs)

        weight_spec = pl.BlockSpec(
            (self.group, self.slots, self.blk, self.blk), lambda g: (g, 0, 0, 0)
        )
        return call(
            body,
            (self.steps,),
            [whole(acts.shape)]
            + [by_cols(self.rows, self.width)] * n_far
            + [weight_spec]
            + self.code_specs(codes)
            + [by_cols(self.rank, self.width)]
            + extra_specs,
            outs,
            out_shapes,
            scratch,
            self.flops(self.slots + 2),
            (acts, *far_acts, weights, *(value for value, _ in codes), v, *extra),
            name,
            after,
        )

    def hidden(self, inputs, far_inputs, w_in, codes, v_in, u_out, after=()):
        def finish(g, j, pre, refs):
            u_ref, act_ref, slope_ref, code_ref, sum_ref = refs
            active, slope = gelu_parts(pre)
            act = active.astype(BF16)
            act_ref[:, self.cut(j)] = act
            slope_ref[:, self.cut(j)] = slope
            part = dot(act, u_ref[self.cut(j), :])
            if j == 0:
                sum_ref[...] = jnp.where(g == 0, part, sum_ref[...] + part)
            else:
                sum_ref[...] += part
            if j == self.group - 1:
                code_ref[...] = sum_ref[...].astype(BF16)

        return self.forward(
            inputs,
            far_inputs,
            w_in,
            codes,
            v_in,
            finish,
            [by_cols(self.rows, self.width)] * 2 + [whole((self.rows, self.rank))],
            [
                shape_of((self.rows, self.cols)),
                shape_of((self.rows, self.cols), F32),
                shape_of((self.rows, self.rank)),
            ],
            [u_out],
            [by_rows(self.width, self.rank)],
            [pltpu.VMEM((self.rows, self.rank), F32)],
            "hidden",
            after,
        )

    def result(self, act, far_acts, w_out, codes, v_out, after=()):
        def finish(g, j, total, refs):
            refs[0][:, self.cut(j)] = total.astype(BF16)

        return self.forward(
            act,
            far_acts,
            w_out,
            codes,
            v_out,
            finish,
            [by_cols(self.rows, self.width)],
            [shape_of((self.rows, self.cols))],
            [],
            [],
            [],
            "result",
            after,
        )[0]

    def backward(self, grads, weights, codes, u, far_parts, finish, outs, out_shapes, extra, extra_specs, scratch, name, after=()):
        n_far, n_codes, n_extra = len(far_parts), len(codes), len(extra)

        def body(g_ref, w_ref, *refs):
            code_refs, refs = refs[:n_codes], refs[n_codes:]
            u_ref, refs = refs[0], refs[1:]
            far_refs, refs = refs[:n_far], refs[n_far:]
            g = pl.program_id(0)
            code = self.code_of(code_refs)
            for j in range(self.group):
                places = [self.place(g, j, k) for k in range(1 + self.local)]
                stacked = jnp.concatenate(
                    [self.columns(g_ref, place) for place in places] + [code], axis=1
                )
                weight = jnp.concatenate(
                    [w_ref[place, k] for k, place in enumerate(places)] + [u_ref[self.cut(j), :]],
                    axis=1,
                )
                total = dot_nt(stacked, weight)
                for ref in far_refs:
                    total = total + ref[:, self.cut(j)].astype(F32)
                finish(g, j, total, refs)

        return call(
            body,
            (self.steps,),
            [whole(grads.shape), whole(weights.shape)]
            + self.code_specs(codes)
            + [by_rows(self.width, self.rank)]
            + [by_cols(self.rows, self.width)] * n_far
            + extra_specs,
            outs,
            out_shapes,
            scratch,
            self.flops(2 + self.local),
            (grads, weights, *(value for value, _ in codes), u, *far_parts, *extra),
            name,
            after,
        )

    def hidden_grad(self, cotangent, w_out, backs, u_out, far_parts, slope, v_in, w_in, code_part, cut, after=()):
        def finish(g, j, total, refs):
            s_ref, v_ref, w_ref, c_ref, pg_ref, code_ref = refs[:6]
            outs = refs[6 : 6 + 2 * self.far]
            sum_ref = refs[-1]
            grad = (total * s_ref[:, self.cut(j)]).astype(BF16)
            pg_ref[:, self.cut(j)] = grad
            for k in range(self.far):
                part = dot_nt(grad, w_ref[j, 1 + self.local + k]).astype(BF16)
                outs[k][:, self.cut(j)] = part[:cut]
                outs[self.far + k][:, self.cut(j)] = part[cut:]
            part = dot_nt(grad, v_ref[:, self.cut(j)])
            if j == 0:
                sum_ref[...] = jnp.where(g == 0, part, sum_ref[...] + part)
            else:
                sum_ref[...] += part
            if j == self.group - 1:
                code_ref[: self.rows] = c_ref[...]
                code_ref[self.rows :] = sum_ref[...].astype(BF16)

        weight_spec = pl.BlockSpec(
            (self.group, self.slots, self.blk, self.blk), lambda g: (g, 0, 0, 0)
        )
        got = self.backward(
            cotangent,
            w_out,
            backs,
            u_out,
            far_parts,
            finish,
            [by_cols(self.rows, self.width), whole((2 * self.rows, self.rank))]
            + [by_cols(cut, self.width)] * self.far
            + [by_cols(self.rows - cut, self.width)] * self.far,
            [shape_of((self.rows, self.cols)), shape_of((2 * self.rows, self.rank))]
            + [shape_of((cut, self.cols))] * self.far
            + [shape_of((self.rows - cut, self.cols))] * self.far,
            [slope, v_in, w_in, code_part],
            [
                by_cols(self.rows, self.width),
                by_cols(self.rank, self.width),
                weight_spec,
                whole(code_part.shape),
            ],
            [pltpu.VMEM((self.rows, self.rank), F32)],
            "hidden_grad",
            after,
        )
        return got[0], got[1], (got[2 : 2 + self.far], got[2 + self.far :])

    def input_grad(self, pre_grad, w_in, backs, u_in, after=()):
        def finish(g, j, total, refs):
            refs[0][:, self.cut(j)] = total

        return self.backward(
            pre_grad,
            w_in,
            backs,
            u_in,
            [],
            finish,
            [by_cols(self.rows, self.width)],
            [shape_of((self.rows, self.cols), F32)],
            [],
            [],
            [],
            "input_grad",
            after,
        )[0]

    def weight_grads(self, cuts, grads, acts=None, far_acts=(), codes=(), backs=(), u_acts=None, after=()):
        spot, n_tok, n_sub = cuts
        height = self.blk // (n_tok * n_sub)
        n_local = 0 if acts is None else 1 + self.local
        n_stack = n_local + len(far_acts) + (1 if codes else 0)
        parts = n_stack + (1 if backs else 0)

        def body(spot_ref, *refs):
            refs = list(refs)
            take = lambda count: [refs.pop(0) for _ in range(count)]
            (g_ref,) = take(1)
            acts_ref = take(0 if acts is None else 1)
            far_refs = take(len(far_acts))
            code_refs, back_refs = take(len(codes)), take(len(backs))
            u_ref = take(1 if backs else 0)
            outs, hold = refs[:n_sub], refs[n_sub]
            g = pl.program_id(0)
            code, back = self.code_of(code_refs), self.code_of(back_refs)
            for j in range(self.group):
                pieces = [self.columns(acts_ref[0], self.place(g, j, k)) for k in range(n_local)]
                pieces += [ref[:, self.cut(j)] for ref in far_refs]
                pieces += [code] if codes else []
                grad = g_ref[:, self.cut(j)]
                hold[:n_stack] = dot_tn(jnp.concatenate(pieces, axis=1), grad).reshape(
                    n_stack, self.blk, self.blk
                )
                if backs:
                    hold[n_stack] = dot_tn(back, u_ref[0][:, self.cut(j)])
                for m in range(n_tok):
                    for h in range(n_sub):
                        first = ((spot_ref[0] ^ m) * n_sub + (spot_ref[1] ^ h)) * height
                        outs[h][m, j] = hold[
                            :, pl.ds(pl.multiple_of(first, height), height), :
                        ].astype(BF16)

        shape = (n_tok, self.blocks, parts, height, self.blk)
        spec = pl.BlockSpec(
            (n_tok, self.group, parts, height, self.blk), lambda g: (0, g, 0, 0, 0)
        )
        cols = by_cols(self.rows, self.width)
        return call(
            body,
            (self.steps,),
            [pl.BlockSpec(memory_space=pltpu.SMEM), cols]
            + ([] if acts is None else [whole(acts.shape)])
            + [cols] * len(far_acts)
            + self.code_specs(codes)
            + self.code_specs(backs)
            + ([cols] if backs else []),
            [spec] * n_sub,
            [shape_of(shape)] * n_sub,
            [pltpu.VMEM((parts, self.blk, self.blk), F32)],
            self.flops(parts),
            [spot, grads]
            + ([] if acts is None else [acts])
            + list(far_acts)
            + [value for value, _ in (*codes, *backs)]
            + ([u_acts] if backs else []),
            "weight_grads",
            after,
        )

    def core_sums(self, kept, got, after=()):
        n_tok, blocks, parts, height, blk = kept.shape
        others = n_tok - 1

        def body(*refs):
            ins, outs = refs[: len(refs) - others], refs[len(refs) - others :]
            for m in range(others):
                outs[m][...] = sum(ref[1 + m].astype(F32) for ref in ins).astype(BF16)

        spec_in = pl.BlockSpec((n_tok, self.group, parts, height, blk), lambda g: (0, g, 0, 0, 0))
        spec_out = pl.BlockSpec((self.group, parts, height, blk), lambda g: (g, 0, 0, 0))
        return call(
            body,
            (self.steps,),
            [spec_in] * (1 + len(got)),
            [spec_out] * others,
            [shape_of((blocks, parts, height, blk))] * others,
            [],
            0,
            (kept, *got),
            "core_sums",
            after,
        )

    def last_sums(self, sums, targets, after=()):
        sizes = [1 + len(got) + len(arrived) for _, got, arrived in sums]
        near = [1 + len(got) for _, got, _ in sums]
        height, blk = sums[0][0].shape[3:]

        def body(*refs):
            ins, outs = refs[: sum(sizes)], refs[sum(sizes) :]
            for j in range(self.group):
                totals, at = [], 0
                for size, count in zip(sizes, near):
                    totals.append(
                        sum(
                            (ref[0, j] if i < count else ref[j]).astype(F32)
                            for i, ref in enumerate(ins[at : at + size])
                        )
                    )
                    at += size
                for target, ref in zip(targets, outs):
                    if isinstance(target, list):
                        to = 0
                        for which, first, count in target:
                            ref[j, to : to + count] = totals[which][first : first + count]
                            to += count
                    else:
                        ref[:, self.cut(j)] = totals[target[0]][target[1]]

        ins, args = [], []
        for kept, got, arrived in sums:
            n_tok, blocks, parts = kept.shape[:3]
            spec_near = pl.BlockSpec(
                (1, self.group, parts, height, blk), lambda g: (0, g, 0, 0, 0)
            )
            spec_far = pl.BlockSpec((self.group, parts, height, blk), lambda g: (g, 0, 0, 0))
            ins += [spec_near] * (1 + len(got)) + [spec_far] * len(arrived)
            args += [kept, *got, *arrived]
        outs, shapes = [], []
        for target in targets:
            if isinstance(target, list):
                count = sum(c for _, _, c in target)
                outs.append(pl.BlockSpec((self.group, count, height, blk), lambda g: (g, 0, 0, 0)))
                shapes.append(shape_of((self.blocks, count, height, blk), F32))
            else:
                outs.append(by_cols(height, self.width))
                shapes.append(shape_of((height, self.cols), F32))
        return call(body, (self.steps,), ins, outs, shapes, [], 0, args, "last_sums", after)

    def final(self, local, far_parts, first, total=None):
        height = far_parts[0].shape[0]
        count = 0 if total is None else 1

        def body(*refs):
            refs = refs[count:]
            value = refs[0][...]
            for ref in refs[1:-1]:
                value = value + ref[...].astype(F32)
            refs[-1][...] = value.astype(BF16)

        rows = pl.BlockSpec((height, self.width), lambda g: (first // height, g))
        return pl.pallas_call(
            body,
            grid=(self.steps,),
            in_specs=[pl.BlockSpec(memory_space=pl.ANY)] * count
            + [rows]
            + [by_cols(height, self.width)] * len(far_parts),
            out_specs=rows,
            out_shape=shape_of((self.rows, self.cols)),
            input_output_aliases={0: 0} if count else {},
            compiler_params=pltpu.CompilerParams(vmem_limit_bytes=24 * 1024 * 1024),
            name="final",
        )(*([total] if count else []), local, *far_parts)


def shards(inputs, cotangent, w_in, w_out, u_in, v_in, u_out, v_out):
    layer = Layer(inputs, w_in)
    n_feat, n_tok, n_sub = (lax.axis_size(name) for name in ("feat", "tok", "sub"))
    spot = jnp.stack([lax.axis_index("tok"), lax.axis_index("sub")]).astype(jnp.int32)
    cuts = (spot, n_tok, n_sub)

    def to_partners(values):
        sent = [exchange(value, "feat", 1 << k) for k, value in reversed(list(enumerate(values)))]
        return sent[::-1]

    def add(parts):
        return (parts[0].astype(F32) + parts[1].astype(F32)).astype(BF16)

    def by_levels(part):
        parts = [part, exchange(part, "feat", 1)]
        for level in range(1, n_feat.bit_length() - 2):
            part = add(parts)
            parts = [part, exchange(part, "feat", 1 << level)]
        return add(parts)

    def last_level(part):
        return [part, exchange(part, "feat", n_feat // 2)]

    def halves(parts):
        return [(value, 0) for value in parts], [(value, 1) for value in parts]

    def block(work, *args):
        shapes = jax.eval_shape(work, *args)
        empty = lambda *_: jax.tree.map(lambda x: jnp.zeros(x.shape, x.dtype), shapes)
        return lax.cond(lax.axis_index("feat") < n_feat, work, empty, *args)

    def by_cores(parts):
        kept = parts[0]
        got = [exchange(parts[h], "sub", h) for h in range(1, n_sub)]
        return kept, got, list(layer.core_sums(kept, got)) if n_tok > 1 else []

    def by_chips(kept, got, sums):
        return kept, got, [exchange(value, "tok", 1 + m) for m, value in enumerate(sums)]

    def summed(parts):
        return by_chips(*by_cores(parts))

    cut = layer.rows * 3 // 4

    def start_step(inputs, cotangent, w_out, u_in, v_out):
        products = layer.far_products(cotangent, w_out)
        return products, by_levels(layer.first_codes(inputs, cotangent, u_in, v_out))

    def hidden_step(inputs, cotangent, w_in, v_in, u_out, far_inputs, first):
        codes, backs = halves(first)
        act, slope, code = layer.hidden(inputs, far_inputs, w_in, codes, v_in, u_out)
        parts = layer.weight_grads(cuts, cotangent, acts=act, backs=backs, u_acts=act)
        return act, slope, code, by_cores(parts)

    def grad_step(
        inputs, cotangent, w_in, w_out, v_in, u_out, far_inputs, far_cot, slope, code, first, done
    ):
        codes, backs = halves(first)
        pre_grad, code, products = layer.hidden_grad(
            cotangent, w_out, backs, u_out, far_cot, slope, v_in, w_in, code, cut, after=done
        )
        parts = layer.weight_grads(cuts, pre_grad, acts=inputs, far_acts=far_inputs, codes=codes)
        return pre_grad, last_level(by_levels(code)), products, summed(parts)

    def last_step(inputs, cotangent, w_out, v_out, act, far_acts, last):
        codes, backs = halves(last)
        parts = layer.weight_grads(
            cuts, cotangent, far_acts=far_acts, codes=codes, backs=backs, u_acts=inputs
        )
        output = layer.result(act, far_acts, w_out, codes, v_out, after=parts[:1])
        return output, summed(parts)

    far_inputs = to_partners([inputs] * layer.far)
    products, first = block(start_step, inputs, cotangent, w_out, u_in, v_out)
    first = last_level(first)
    far_cot = to_partners(products)
    act, slope, code, sums_early = block(
        hidden_step, inputs, cotangent, w_in, v_in, u_out, far_inputs, first
    )
    far_acts = to_partners([act] * layer.far)
    sums_early = by_chips(*sums_early)
    pre_grad, last, products, sums_in = block(
        grad_step,
        inputs, cotangent, w_in, w_out, v_in, u_out, far_inputs, far_cot, slope, code, first,
        sums_early[2],
    )
    ready = pin([*products[0], *products[1]], *far_acts)
    far_pre = to_partners(ready[: layer.far])
    far_rest = to_partners(ready[layer.far :])
    output, sums_late = block(
        last_step, inputs, cotangent, w_out, v_out, act, far_acts, last
    )
    near, slots = 1 + layer.local, layer.slots
    grad_w_in, grad_v_in = layer.last_sums(
        [sums_in], [[(0, 0, slots)], (0, slots)], after=[output]
    )
    grad_w_out, grad_u_out, grad_v_out, grad_u_in = layer.last_sums(
        [sums_early, sums_late],
        [[(0, 0, near), (1, 0, layer.far)], (0, near), (1, layer.far), (1, layer.far + 1)],
    )
    local_grad = layer.input_grad(pre_grad, w_in, halves(last)[1], u_in, after=[grad_v_out])
    in_grad = layer.final(local_grad, far_rest, cut, layer.final(local_grad, far_pre, 0))
    return (
        output,
        in_grad,
        grad_w_in,
        grad_w_out,
        grad_u_in.T,
        grad_v_in,
        grad_u_out.T,
        grad_v_out,
    )


def solution(mesh):
    placed = (
        P(("group", "tok", "sub"), "feat"),
        P(("group", "tok", "sub"), "feat"),
        P("feat", None, None, None),
        P("feat", None, None, None),
        P("feat", None),
        P(None, "feat"),
        P("feat", None),
        P(None, "feat"),
    )
    return jax.shard_map(
        shards,
        mesh=mesh,
        in_specs=placed,
        out_specs=(
            P(("group", "tok", "sub"), "feat"),
            P(("group", "tok", "sub"), "feat"),
            P(("group", "feat"), None, ("tok", "sub"), None),
            P(("group", "feat"), None, ("tok", "sub"), None),
            P(("group", "feat"), ("tok", "sub")),
            P(("group", "tok", "sub"), "feat"),
            P(("group", "feat"), ("tok", "sub")),
            P(("group", "tok", "sub"), "feat"),
        ),
        check_vma=False,
    )
```
